128 devices in a mesh: sfc: 8 (over x, core), node: 16 (over z, y).
Axes of the slice: x: 4, y: 4, z: 4, core: 2. Of those that a mesh axis runs over, the one named last changes fastest.
Arguments:
- fine_state: float32 [128, 21, 32, 1024], P(('sfc', 'node')), may hold values from -6 to 6
- conduct: float32 [128, 32, 1024], P(('sfc', 'node')), may hold values from 0.2 to 2
- spec_rate: float32 [21], replicated, may hold values from 0.1 to 1
- reaction: float32 [21, 21], replicated, may hold values from -2 to 2
- coarse_state: float32 [128, 21, 32, 1024], P(('sfc', 'node')), may hold values from -6 to 6
- ghost_source: int32 [128, 6], P(('sfc', 'node')), may hold values from -1 to 287, as said below
- parent_box: int32 [128], P(('sfc', 'node')), may hold values from 0 to 127
Outputs:
- tendency: float32 [128, 21, 32, 1024], P(('sfc', 'node'))
- register: float32 [128, 48, 21, 256], P(('sfc', 'node'))
The draws below stay inside these ranges and needn't reach their ends.
Inputs may be any that keep to these rules, and one draw needn't show every extreme that they name: ghost_source is -1 on about a third of the faces; box 0 names the largest index on face 0 and is coarse-fine on face 1.
All inputs are finite; a program needn't handle non-finite values.
Results may differ from the reference program's by a relative error of at most 0.0003.
Values sent between devices are 32-bit elements; how exact they have to be, the bound alone decides.
No kernel may reach another device: no remote copies, remote signals or barrier semaphores. Data moves between devices by JAX's collectives and lax.ppermute only.
A program may use at most 256 MiB of HBM per device.

```python
import math
import jax
import jax.numpy as jnp
from jax import lax

B = 32
S = 21
BOX_CAP = 1
COARSE_DEV = 1
BOXES = 128
COARSE_BOXES = 128
N_SFC = 8
N_NODE = 16


def draw_ghost_source(key, part):
    key = jax.random.fold_in(key, 11)
    first, second = jax.random.split(key)
    top = 3 * N_NODE * BOX_CAP * 6
    values = jax.random.randint(first, (BOXES, 6), 0, top)
    coarse = jax.random.randint(second, (BOXES, 6), 0, 3) == 0
    values = jnp.where(coarse, -1, values)
    values = values.at[0, 0].set(top - 1).at[0, 1].set(-1)
    return values.astype(jnp.int32)


def touch_ends(array, rng, smallest, largest):
    extent = array.shape
    place = [jax.random.randint(jax.random.fold_in(rng, axis), (), 0, extent[axis]) for axis in range(len(extent))]
    array = array.at[tuple(place)].set(smallest)
    longest = extent.index(max(extent))
    place[longest] = (place[longest] + 1) % extent[longest]
    return array.at[tuple(place)].set(largest)


def levels(rng, extent, pieces, least, top_value):
    loudness = 1.0
    for position, shards_of in pieces:
        steps = jax.random.uniform(jax.random.fold_in(jax.random.fold_in(rng, 6), position), (shards_of,), jnp.float32, least / len(pieces), top_value / len(pieces))
        loudness = loudness * jnp.repeat(jnp.exp(steps), extent[position] // shards_of).reshape((-1,) + (1,) * (len(extent) - 1 - position))
    return loudness


def scatter_about(key, shape, scale, most, cuts=(), kind=jnp.bfloat16):
    entries = jax.random.normal(key, shape, jnp.float32) * scale
    if len(cuts) > 0:
        entries = levels(key, shape, cuts, -0.22, 0.18) * entries
    return jnp.clip(entries, min=-most, max=most).astype(kind)


def setup_inputs(seed: int = 0) -> dict:
    key_of = jax.random.split(jax.random.key(seed), 8)
    fine_state = scatter_about(key_of[0], (BOXES, S, B, B * B), 1.0, 6.0, ((0, 128),), jnp.float32)
    conduct = jnp.clip(jnp.exp(math.log(2.0) - 2.3025851 * jax.random.uniform(key_of[1], (BOXES, B, B * B), jnp.float32) ** levels(key_of[1], (BOXES, B, B * B), ((0, 128),), -0.2, 0.2)), 0.2, 2.0)
    spec_rate = jnp.clip(jnp.exp(jax.random.uniform(key_of[2], (S,), jnp.float32, math.log(0.1), math.log(1.0))), 0.1, 1.0)
    reaction = scatter_about(key_of[3], (S, S), 0.3, 2.0, (), jnp.float32)
    coarse_state = scatter_about(key_of[4], (COARSE_BOXES, S, B, B * B), 1.0, 6.0, ((0, 128),), jnp.float32)
    ghost_source = draw_ghost_source(jax.random.fold_in(key_of[7], 71), 0)
    parent_box = touch_ends(jax.random.randint(key_of[6], (BOXES,), 0, N_NODE * COARSE_DEV * 8), jax.random.fold_in(key_of[6], 1), 0, (N_NODE * COARSE_DEV * 8) - 1).astype(jnp.int32)
    return {"fine_state": fine_state, "conduct": conduct, "spec_rate": spec_rate, "reaction": reaction, "coarse_state": coarse_state, "ghost_source": ghost_source, "parent_box": parent_box}


def faces_of(field):
    chans, side = field.shape[0], field.shape[1]
    cube = field.reshape(chans, side, side, side)
    slabs = [cube[:, 0], cube[:, -1], cube[:, :, 0, :], cube[:, :, -1, :], cube[:, :, :, 0], cube[:, :, :, -1]]
    return jnp.stack([s.reshape(chans, side * side) for s in slabs], 0)


def coarse_faces(coarse):
    chans, side = coarse.shape[0], coarse.shape[1]
    half = side // 2
    cube = coarse.reshape(chans, 2, half, 2, half, 2, half).transpose(1, 3, 5, 0, 2, 4, 6).reshape(8, chans, half, half, half)
    slabs = [cube[:, :, 0], cube[:, :, -1], cube[:, :, :, 0], cube[:, :, :, -1], cube[:, :, :, :, 0], cube[:, :, :, :, -1]]
    return jnp.stack(slabs, 1).reshape(8, 6, chans, half * half)


def expand_coarse(slabs, side):
    half = side // 2
    lead = slabs.shape[:-1]
    grid = slabs.reshape(lead + (half, half))
    grid = jnp.repeat(jnp.repeat(grid, 2, axis=-2), 2, axis=-1)
    return grid.reshape(lead + (side * side,))


def box_step(state, kappa, ghosts, spec_rate, reaction):
    chans, side = state.shape[0], state.shape[1]
    area = side * side
    slabs = ghosts.reshape(6, chans, side, side)
    zpos = jnp.arange(area, dtype=jnp.int32) % side
    first = (zpos == 0)[None, None, :]
    last = (zpos == side - 1)[None, None, :]
    zero_col = jnp.zeros((chans, side, 1), jnp.float32)
    near = [
        jnp.concatenate([ghosts[0].reshape(chans, 1, area), state[:, :-1]], 1),
        jnp.concatenate([state[:, 1:], ghosts[1].reshape(chans, 1, area)], 1),
        jnp.concatenate([slabs[2], state[:, :, :-side]], 2),
        jnp.concatenate([state[:, :, side:], slabs[3]], 2),
        jnp.where(first, jnp.repeat(slabs[4], side, axis=2), jnp.concatenate([zero_col, state[:, :, :-1]], 2)),
        jnp.where(last, jnp.repeat(slabs[5], side, axis=2), jnp.concatenate([state[:, :, 1:], zero_col], 2)),
    ]
    kfirst = (zpos == 0)[None, :]
    klast = (zpos == side - 1)[None, :]
    kappa_near = [
        jnp.concatenate([kappa[:1], kappa[:-1]], 0),
        jnp.concatenate([kappa[1:], kappa[-1:]], 0),
        jnp.concatenate([kappa[:, :side], kappa[:, :-side]], 1),
        jnp.concatenate([kappa[:, side:], kappa[:, -side:]], 1),
        jnp.where(kfirst, kappa, jnp.concatenate([kappa[:, :1], kappa[:, :-1]], 1)),
        jnp.where(klast, kappa, jnp.concatenate([kappa[:, 1:], kappa[:, -1:]], 1)),
    ]
    spread = jnp.zeros_like(state)
    for value, other in zip(near, kappa_near):
        spread = spread + (0.5 * (kappa + other))[None] * (value - state)
    source = jnp.einsum("st,txc->sxc", reaction, state, precision=lax.Precision.HIGHEST)
    tendency = spec_rate[:, None, None] * spread + source
    inner = faces_of(state)
    kappa_face = faces_of(kappa[None])[:, 0]
    flux = spec_rate[None, :, None] * kappa_face[:, None, :] * (inner - ghosts)
    half = side // 2
    coarse_flux = flux.reshape(6, chans, half, 2, half, 2).mean(axis=(3, 5)).reshape(6, chans, half * half)
    return tendency, coarse_flux


def reference(fine_state, conduct, spec_rate, reaction, coarse_state, ghost_source, parent_box):
    chans, side = fine_state.shape[1], fine_state.shape[2]
    area = side * side
    half = side // 2
    group = N_NODE * BOX_CAP * 6
    cgroup = N_NODE * COARSE_DEV * 8
    all_faces = lax.map(faces_of, fine_state).reshape(N_SFC, group, chans, area)
    padded = jnp.concatenate([jnp.zeros((1, group, chans, area), jnp.float32), all_faces, jnp.zeros((1, group, chans, area), jnp.float32)], 0)
    ctab = lax.map(coarse_faces, coarse_state).reshape(N_SFC, cgroup, 6, chans, half * half)
    curve = (jnp.arange(BOXES, dtype=jnp.int32) // BOX_CAP) // N_NODE

    def one_box(items):
        state, kappa, source, parent, sidx = items
        safe = jnp.maximum(source, 0)
        near = padded[sidx + safe // group, safe % group]
        from_coarse = expand_coarse(ctab[sidx, parent], side)
        ghosts = jnp.where((source >= 0)[:, None, None], near, from_coarse)
        return box_step(state, kappa, ghosts, spec_rate, reaction)

    tendency, coarse_flux = lax.map(one_box, (fine_state, conduct, ghost_source, parent_box, curve))
    mask = (ghost_source < 0).astype(jnp.float32)
    terms = coarse_flux * mask[:, :, None, None]
    rows = (curve[:, None] * cgroup + parent_box[:, None]) * 6 + jnp.arange(6, dtype=jnp.int32)[None, :]
    register = jax.ops.segment_sum(terms.reshape(BOXES * 6, chans, half * half), rows.reshape(-1), num_segments=COARSE_BOXES * 48)
    return tendency, register.reshape(COARSE_BOXES, 48, chans, half * half)
```

```python
import functools

import jax
import jax.numpy as jnp
import numpy as np
from jax import lax
from jax.experimental import pallas as pl
from jax.experimental.pallas import tpu as pltpu
from jax.sharding import PartitionSpec as P

S, B, AREA = 21, 32, 1024
PIECES = 16
HALF = 11
SLOTS = 24
ROWS = 12
FINE = 6 * ROWS
CROWS = 16
F32, BF16 = jnp.float32, jnp.bfloat16


def slot(s):
    return s if s < HALF else s + 1


def pick_fine():
    m = np.zeros((AREA, 128), np.float32)
    for b in range(32):
        m[b, b] = 1
        m[31 * 32 + b, 32 + b] = 1
        m[b * 32, 64 + b] = 1
        m[b * 32 + 31, 96 + b] = 1
    return m


def pick_coarse():
    m = np.zeros((AREA, 256), np.float32)
    for w, p in enumerate((0, 15, 16, 31)):
        for b in range(32):
            m[p * 32 + b, w * 32 + b] = 1
            m[b * 32 + p, 128 + w * 32 + b] = 1
    return m


def split_octants():
    m = np.zeros((256, 256), np.float32)
    for a in range(8):
        for o in range(2):
            for b in range(16):
                m[a * 32 + o * 16 + b, o * 128 + a * 16 + b] = 1
    return m


def average():
    m = np.zeros((512, 128), np.float32)
    for a in range(16):
        for b in range(32):
            m[a * 32 + b, (a // 2) * 16 + b // 2] = 0.25
    return m


def dot(x, m):
    hi = x.astype(BF16)
    lo = (x - hi.astype(F32)).astype(BF16)
    return jnp.dot(hi, m, preferred_element_type=F32) + jnp.dot(lo, m, preferred_element_type=F32)


def lanes(rows):
    return lax.broadcasted_iota(jnp.int32, (rows, 128), 1)


def swap_blocks(parts):
    block = lanes(parts[0].shape[0]) // 32
    out = []
    for f in range(4):
        acc = None
        for q in range(4):
            moved = parts[q] if q == f else pltpu.roll(parts[q], (32 * (q - f)) % 128, 1)
            acc = moved if acc is None else jnp.where(block == q, moved, acc)
        out.append(acc)
    return out


def pack_fine_kernel(source, parent, state, conduct, rate, pick, mean, fine, means, edge, xs, weighted, mr, nr):
    edge[HALF * 32 : HALF * 32 + 32, :] = jnp.zeros((32, 128), F32)
    edge[22 * 32 : 23 * 32, :] = jnp.zeros((32, 128), F32)
    xs[...] = jnp.zeros_like(xs)
    sel = pick[...]
    for lo, hi in ((0, 6), (6, 11), (11, 16), (16, 21)):
        got = dot(state[0, lo:hi].reshape((hi - lo) * 32, AREA), sel)
        edge[slot(lo) * 32 : (slot(lo) + hi - lo) * 32, :] = got
    edge[23 * 32 : 24 * 32, :] = dot(conduct[0], sel)
    for s in range(S):
        xs[0, slot(s) : slot(s) + 1, :] = state[0, s, 0:1, :]
        xs[1, slot(s) : slot(s) + 1, :] = state[0, s, 31:32, :]
    xs[0, 23:24, :] = conduct[0, 0:1, :]
    xs[1, 23:24, :] = conduct[0, 31:32, :]
    row = lax.broadcasted_iota(jnp.int32, (SLOTS, 128), 0)
    rates = jnp.broadcast_to(rate[...], (SLOTS, 128))
    for k in range(8):
        across = [xs[side, :, 128 * k : 128 * k + 128] for side in range(2)]
        across += swap_blocks([edge[pl.ds(4 * k + q, SLOTS, stride=32), :] for q in range(4)])
        k2, kk = k // 4, k % 4
        for f in range(6):
            t = across[f]
            fine[2 * k, f * ROWS : (f + 1) * ROWS, :] = t[:ROWS]
            fine[2 * k + 1, f * ROWS : (f + 1) * ROWS, :] = t[ROWS:]
            kap = jnp.broadcast_to(t[23:24], (SLOTS, 128))
            at = (f * 2 + k2) * SLOTS
            weighted[at : at + SLOTS, 128 * kk : 128 * kk + 128] = jnp.where(row == 23, t, t * kap * rates)
    lane = lanes(1)
    note = jnp.where(lane == 6, parent[0], 0)
    for f in range(6):
        note = jnp.where(lane == f, source[0, f], note)
    fine[:, 11:12, :] = jnp.broadcast_to(note.astype(F32)[None], (PIECES, 1, 128))
    averaged = dot(weighted[...], mean[...])
    mr[...] = jnp.zeros_like(mr)
    nr[...] = jnp.zeros_like(nr)
    for f in range(6):
        keep = jnp.where(source[0, f] < 0, 1.0, 0.0).astype(F32)
        for k2 in range(2):
            fk = f * 2 + k2
            first = averaged[fk * SLOTS : (fk + 1) * SLOTS] * keep
            second = jnp.broadcast_to(first[23:24], (SLOTS, 128)) * rates
            for ref, v in ((mr, first), (nr, second)):
                ref[fk * S : fk * S + HALF, :] = v[:HALF]
                ref[fk * S + HALF : (fk + 1) * S, :] = v[ROWS : ROWS + S - HALF]
    for j in range(PIECES):
        means[j, :CROWS, :] = mr[j * CROWS : (j + 1) * CROWS, :]
        means[j, CROWS:, :] = nr[j * CROWS : (j + 1) * CROWS, :]


def turn(x):
    n = x.shape[0] // 8
    x = x.reshape(n, 8, 128)
    row = lax.broadcasted_iota(jnp.int32, (n, 8, 128), 1)
    group = lax.broadcasted_iota(jnp.int32, (n, 8, 128), 2) // 16
    for d in (1, 2, 4):
        up = pltpu.roll(pltpu.roll(x, 8 - d, 1), 16 * d, 2)
        down = pltpu.roll(pltpu.roll(x, d, 1), 128 - 16 * d, 2)
        rb, gb = row & d, group & d
        x = jnp.where(rb == gb, x, jnp.where(rb == 0, up, down))
    return x.reshape(n * 8, 128)


def pack_coarse_kernel(coarse, means, pick, octs, out, turned, planes, table):
    sel = pick[...]
    for lo in range(0, S, 7):
        got = dot(coarse[0, lo : lo + 7].reshape(224, AREA), sel)
        turned[0, lo * 32 : (lo + 7) * 32, :] = got[:, :128]
        turned[1, lo * 32 : (lo + 7) * 32, :] = got[:, 128:]
    for t in range(2):
        for lo in range(S):
            turned[t, lo * 32 : (lo + 1) * 32, :] = turn(turned[t, lo * 32 : (lo + 1) * 32, :])
    planes[...] = jnp.zeros_like(planes)
    for w, p in enumerate((0, 15, 16, 31)):
        for s in range(S):
            planes[w * SLOTS + s : w * SLOTS + s + 1, :] = coarse[0, s, p : p + 1, :]
    for o in range(8):
        table[o, 12 * S :, :] = jnp.zeros((256 - 12 * S, 128), F32)
    for oy in range(2):
        for k2 in range(2):
            c = oy * 2 + k2
            got = dot(planes[:, 256 * c : 256 * c + 256], octs[...])
            for w in range(4):
                for oz in range(2):
                    o, fk = 4 * (w // 2) + 2 * oy + oz, (w % 2) * 2 + k2
                    table[o, fk * S : (fk + 1) * S, :] = got[w * SLOTS : w * SLOTS + S, oz * 128 : oz * 128 + 128]
    for t in range(2):
        for g in range(4):
            ox, k2 = g // 2, g % 2
            for w in range(4):
                for i in range(2):
                    oy, oz = (w // 2, i) if t == 0 else (i, w // 2)
                    f = 2 + 2 * t + w % 2
                    fk = f * 2 + k2
                    table[4 * ox + 2 * oy + oz, fk * S : (fk + 1) * S, :] = turned[
                        t, pl.ds(g * 8 + w * 2 + i, S, stride=32), :
                    ]
    for j in range(PIECES):
        for o in range(8):
            out[j, o * CROWS : (o + 1) * CROWS, :] = table[o, j * CROWS : (j + 1) * CROWS, :]
        out[j, 8 * CROWS :, :] = means[j]


def inner_kernel(rate, state, conduct, react, out, coef):
    kap = conduct[0]
    react_hi = react[...].astype(BF16)
    react_lo = (react[...] - react_hi.astype(F32)).astype(BF16)
    col = lax.broadcasted_iota(jnp.int32, (B, AREA), 1)
    row = lax.broadcasted_iota(jnp.int32, (B, AREA), 0)
    y, z = col // 32, col % 32
    diag = jnp.zeros((B, AREA), F32)
    for i, (axis, step, at, end) in enumerate(
        ((0, 1, row, 0), (0, B - 1, row, 31), (1, 32, y, 0), (1, AREA - 32, y, 31), (1, 1, z, 0), (1, AREA - 1, z, 31))
    ):
        edge = at == end
        c = 0.5 * (kap + pltpu.roll(kap, step, axis))
        diag = diag + jnp.where(edge, kap, c)
        coef[i] = jnp.where(edge, 0.0, c)
    coef[6] = diag
    for g in range(4):
        x = state[0, :, g * 8 : g * 8 + 8, :].reshape(S * 8, AREA)
        hi = x.astype(BF16)
        lo = (x - hi.astype(F32)).astype(BF16)
        got = jnp.dot(react_hi, hi, preferred_element_type=F32)
        got += jnp.dot(react_hi, lo, preferred_element_type=F32)
        got += jnp.dot(react_lo, hi, preferred_element_type=F32)
        out[0, :, g * 8 : g * 8 + 8, :] = got.reshape(S, 8, AREA)

    def species(s, carry):
        u = state[0, s]
        acc = -coef[6] * u
        for i, (axis, step) in enumerate(((0, 1), (0, B - 1), (1, 32), (1, AREA - 32), (1, 1), (1, AREA - 1))):
            acc = acc + coef[i] * pltpu.roll(u, step, axis)
        out[0, s] = out[0, s] + rate[s] * acc
        return carry

    lax.fori_loop(0, S, species, 0)


def relay_coarse_kernel(note, got, ghosts, register):
    register[...] = jnp.zeros_like(register)
    for n in range(PIECES):
        p = note[n, 6]
        c, o = p // 8, pl.multiple_of((p % 8) * CROWS, CROWS)
        piece = got[c, pl.ds(o, CROWS), :]
        ghosts[n] = piece
        flux = got[n, 8 * CROWS : 9 * CROWS, :] - got[n, 9 * CROWS :, :] * piece
        register[c, pl.ds(o, CROWS), :] = register[c, pl.ds(o, CROWS), :] + flux


def relay_fine_kernel(note, before, own, after, ghosts, out, table):
    for g, ref in enumerate((before, own, after)):
        for n in range(PIECES):
            for f in range(6):
                table[g * 96 + n * 6 + f, :ROWS, :] = ref[n, f * ROWS : (f + 1) * ROWS, :]
    for n in range(PIECES):
        for f in range(6):
            q = jnp.maximum(note[n, f], 0)
            out[n, f * ROWS : (f + 1) * ROWS, :] = table[q, :ROWS, :]
        out[n, FINE:, :] = ghosts[n]


def outer_kernel(rate, source, inner, got, conduct, spread, place, out, crow, cslot, wide, xs, edge):
    for j in range(PIECES):
        crow[j * CROWS : (j + 1) * CROWS, :] = got[j, FINE:, :]
    cslot[...] = jnp.zeros_like(cslot)
    for fk in range(12):
        cslot[fk * SLOTS : fk * SLOTS + HALF, :] = crow[fk * S : fk * S + HALF, :]
        cslot[fk * SLOTS + ROWS : fk * SLOTS + ROWS + S - HALF, :] = crow[fk * S + HALF : (fk + 1) * S, :]
    wide[...] = dot(cslot[...], spread[...])
    for k in range(8):
        k2, kk = k // 4, k % 4
        slabs = []
        for f in range(6):
            fine = jnp.concatenate(
                [got[2 * k, f * ROWS : (f + 1) * ROWS, :], got[2 * k + 1, f * ROWS : (f + 1) * ROWS, :]], 0
            )
            at = (f * 2 + k2) * SLOTS
            slabs.append(jnp.where(source[0, f] >= 0, fine, wide[at : at + SLOTS, 128 * kk : 128 * kk + 128]))
        for side in range(2):
            xs[side, :, 128 * k : 128 * k + 128] = slabs[side]
        for q, v in enumerate(swap_blocks(slabs[2:])):
            edge[pl.ds(4 * k + q, SLOTS, stride=32), :] = v
    kap = conduct[0]
    row = lax.broadcasted_iota(jnp.int32, (B, AREA), 0)
    for lo, hi in ((0, 6), (6, 11), (11, 16), (16, 21)):
        ghost = dot(edge[slot(lo) * 32 : (slot(lo) + hi - lo) * 32, :], place[...])
        for s in range(lo, hi):
            mine = ghost[(s - lo) * 32 : (s - lo + 1) * 32]
            mine = mine + jnp.where(row == 0, xs[0, slot(s) : slot(s) + 1, :], 0.0)
            mine = mine + jnp.where(row == 31, xs[1, slot(s) : slot(s) + 1, :], 0.0)
            out[0, s] = inner[0, s] + rate[s] * (kap * mine)


def unpack_register_kernel(got, out, table):
    for j in range(PIECES):
        for o in range(8):
            table[o, j * CROWS : (j + 1) * CROWS, :] = got[j, o * CROWS : (o + 1) * CROWS, :]
    for o in range(8):
        for f in range(6):
            for k2 in range(2):
                fk = f * 2 + k2
                out[0, o * 6 + f, :, k2 * 128 : k2 * 128 + 128] = table[o, fk * S : (fk + 1) * S, :]


VM = pl.BlockSpec(memory_space=pltpu.VMEM)
SM = pl.BlockSpec(memory_space=pltpu.SMEM)


def call(kernel, ins, outs, scratch, args, flops=0, limit=40):
    many = isinstance(outs, list)
    shapes = [jax.ShapeDtypeStruct(o, F32) for o in (outs if many else [outs])]
    moved = sum(a.size * a.dtype.itemsize for a in args) + sum(4 * int(np.prod(o.shape)) for o in shapes)
    return pl.pallas_call(
        kernel,
        out_shape=shapes if many else shapes[0],
        in_specs=[SM if c == "s" else VM for c in ins],
        out_specs=[VM] * len(shapes) if many else VM,
        scratch_shapes=[pltpu.VMEM(s, F32) for s in scratch],
        compiler_params=pltpu.CompilerParams(vmem_limit_bytes=limit << 20),
        cost_estimate=pl.CostEstimate(flops=flops, bytes_accessed=moved, transcendentals=0),
        name=kernel.__name__.removesuffix("_kernel"),
    )(*args)


def shifted(block, distance):
    devices = range(lax.axis_size("sfc"))
    return lax.ppermute(block, "sfc", [(i, i + distance) for i in devices if i + distance in devices])


def exchange(block):
    return lax.all_to_all(block, "node", 0, 0, tiled=True)


def local(fine_state, conduct, spec_rate, reaction, coarse_state, ghost_source, parent_box):
    zero = jnp.zeros((1,), F32)
    rates = jnp.concatenate([spec_rate[:HALF], zero, spec_rate[HALF:], zero, zero])[:, None]
    pick = jnp.asarray(pick_fine(), BF16)
    place = jnp.asarray(pick_fine().T, BF16)
    mean = jnp.asarray(average(), BF16)
    spread = jnp.asarray(4 * average().T, BF16)
    fine, means = call(
        pack_fine_kernel,
        "ssvvvvv",
        [(PIECES, FINE, 128), (PIECES, 2 * CROWS, 128)],
        [(SLOTS * 32, 128), (2, SLOTS, AREA), (12 * SLOTS, 512), (256, 128), (256, 128)],
        (ghost_source, parent_box, fine_state, conduct, rates, pick, mean),
        int(1e9),
    )
    own = exchange(fine)
    coarse = call(
        pack_coarse_kernel,
        "vvvv",
        (PIECES, 10 * CROWS, 128),
        [(2, S * 32, 128), (4 * SLOTS, AREA), (8, 256, 128)],
        (coarse_state, means, jnp.asarray(pick_coarse(), BF16), jnp.asarray(split_octants(), BF16)),
        int(1e9),
    )
    grouped = exchange(coarse)
    before, after = shifted(own, 1), shifted(own, -1)
    react = jnp.kron(reaction, jnp.eye(8, dtype=F32))
    inner = call(
        inner_kernel,
        "svvv",
        (1, S, B, AREA),
        [(7, B, AREA)],
        (spec_rate, fine_state, conduct, react),
        int(1e9),
    )
    note = own[:, 11, :8].astype(jnp.int32)
    ghosts, rows = call(
        relay_coarse_kernel,
        "sv",
        [(PIECES, CROWS, 128), (PIECES, 8 * CROWS, 128)],
        [],
        (note, grouped),
    )
    chosen = call(
        relay_fine_kernel,
        "svvvv",
        (PIECES, FINE + CROWS, 128),
        [(3 * 96, ROWS, 128)],
        (note, before, own, after, ghosts),
    )
    mine = exchange(chosen)
    rows = exchange(rows)
    tendency = call(
        outer_kernel,
        "ssvvvvv",
        (1, S, B, AREA),
        [(256, 128), (12 * SLOTS, 128), (12 * SLOTS, 512), (2, SLOTS, AREA), (SLOTS * 32, 128)],
        (spec_rate, ghost_source, inner, mine, conduct, spread, place),
        int(1e9),
    )
    register = call(unpack_register_kernel, "v", (1, 48, S, 256), [(8, 256, 128)], (rows,))
    return tendency, register


def solution(mesh):
    box = P(("sfc", "node"))
    return jax.shard_map(
        local,
        mesh=mesh,
        in_specs=(box, box, P(), P(), box, box, box),
        out_specs=(box, box),
        check_vma=False,
    )
```

```python
import functools

import jax
import jax.numpy as jnp
import numpy as np
from jax import lax
from jax.experimental import pallas as pl
from jax.experimental.pallas import tpu as pltpu
from jax.sharding import PartitionSpec as P

S, B, AREA = 21, 32, 1024
PIECES = 16
HALF = 11
SLOTS = 24
ROWS = 12
FINE = 6 * ROWS
CROWS = 16
F32, BF16 = jnp.float32, jnp.bfloat16


def slot(s):
    return s if s < HALF else s + 1


def pick_fine():
    m = np.zeros((AREA, 128), np.float32)
    for b in range(32):
        m[b, b] = 1
        m[31 * 32 + b, 32 + b] = 1
        m[b * 32, 64 + b] = 1
        m[b * 32 + 31, 96 + b] = 1
    return m


def pick_coarse():
    m = np.zeros((AREA, 256), np.float32)
    for w, p in enumerate((0, 15, 16, 31)):
        for b in range(32):
            m[p * 32 + b, w * 32 + b] = 1
            m[b * 32 + p, 128 + w * 32 + b] = 1
    return m


def split_octants():
    m = np.zeros((256, 256), np.float32)
    for a in range(8):
        for o in range(2):
            for b in range(16):
                m[a * 32 + o * 16 + b, o * 128 + a * 16 + b] = 1
    return m


def average():
    m = np.zeros((512, 128), np.float32)
    for a in range(16):
        for b in range(32):
            m[a * 32 + b, (a // 2) * 16 + b // 2] = 0.25
    return m


def dot(x, m):
    hi = x.astype(BF16)
    lo = (x - hi.astype(F32)).astype(BF16)
    return jnp.dot(hi, m, preferred_element_type=F32) + jnp.dot(lo, m, preferred_element_type=F32)


def lanes(rows):
    return lax.broadcasted_iota(jnp.int32, (rows, 128), 1)


def swap_blocks(parts):
    block = lanes(parts[0].shape[0]) // 32
    out = []
    for f in range(4):
        acc = None
        for q in range(4):
            moved = parts[q] if q == f else pltpu.roll(parts[q], (32 * (q - f)) % 128, 1)
            acc = moved if acc is None else jnp.where(block == q, moved, acc)
        out.append(acc)
    return out


CHUNKS = ((0, 6), (6, 11), (11, 16), (16, 21))


def begin(sems, pairs):
    copies = [pltpu.make_async_copy(src, dst, sems.at[i]) for i, (src, dst) in enumerate(pairs)]
    for c in copies:
        c.start()
    return copies


def pack_fine_kernel(
    source_in, parent_in, state_in, conduct_in, pick_in, mean_in, fine_out, weighted_out,
    source, parent, state, conduct, pick, mean, fine, weighted, edge, xs, kapw, sems,
):
    copies = begin(
        sems,
        [(pick_in, pick), (conduct_in, conduct), (state_in.at[:, 0:6], state.at[:, 0:6])]
        + [(state_in.at[:, lo:hi], state.at[:, lo:hi]) for lo, hi in CHUNKS[1:]]
        + [(mean_in, mean), (source_in, source), (parent_in, parent)],
    )
    edge[HALF * 32 : HALF * 32 + 32, :] = jnp.zeros((32, 128), F32)
    edge[22 * 32 : 23 * 32, :] = jnp.zeros((32, 128), F32)
    for side in range(2):
        for r in (11, 22):
            xs[side, r : r + 1, :] = jnp.zeros((1, AREA), F32)
    kapw[...] = jnp.zeros_like(kapw)
    copies[0].wait()
    copies[1].wait()
    sel = pick[...]
    edge[23 * 32 : 24 * 32, :] = dot(conduct[0], sel)
    xs[0, 23:24, :] = conduct[0, 0:1, :]
    xs[1, 23:24, :] = conduct[0, 31:32, :]
    for i, (lo, hi) in enumerate(CHUNKS):
        copies[2 + i].wait()
        got = dot(state[0, lo:hi].reshape((hi - lo) * 32, AREA), sel)
        edge[slot(lo) * 32 : (slot(lo) + hi - lo) * 32, :] = got
        for s in range(lo, hi):
            xs[0, slot(s) : slot(s) + 1, :] = state[0, s, 0:1, :]
            xs[1, slot(s) : slot(s) + 1, :] = state[0, s, 31:32, :]
    row = lax.broadcasted_iota(jnp.int32, (SLOTS, 128), 0)
    for k in range(8):
        across = [xs[side, :, 128 * k : 128 * k + 128] for side in range(2)]
        across += swap_blocks([edge[pl.ds(4 * k + q, SLOTS, stride=32), :] for q in range(4)])
        k2, kk = k // 4, k % 4
        for f in range(6):
            t = across[f]
            fine[2 * k, f * ROWS : (f + 1) * ROWS, :] = t[:ROWS]
            fine[2 * k + 1, f * ROWS : (f + 1) * ROWS, :] = t[ROWS:]
            at = f * 2 + k2
            kapw[at : at + 1, 128 * kk : 128 * kk + 128] = t[23:24]
            kap = jnp.broadcast_to(t[23:24], (SLOTS, 128))
            weighted[at * SLOTS : (at + 1) * SLOTS, 128 * kk : 128 * kk + 128] = t * kap
    saved = pltpu.make_async_copy(weighted, weighted_out, sems.at[9])
    saved.start()
    for c in copies[6:]:
        c.wait()
    lane = lanes(1)
    note = jnp.where(lane == 6, parent[0], 0)
    for f in range(6):
        note = jnp.where(lane == f, source[0, f], note)
    note = note.astype(F32)
    kmean = dot(kapw[...], mean[...])
    for j in range(PIECES):
        fk = CROWS * j // S
        fk2 = min((CROWS * j + CROWS - 1) // S, 11)
        fine[j, 11:12, :] = note
        fine[j, 23:24, :] = kmean[fk : fk + 1] * jnp.where(source[0, fk // 2] < 0, 1.0, 0.0)
        fine[j, 35:36, :] = kmean[fk2 : fk2 + 1] * jnp.where(source[0, fk2 // 2] < 0, 1.0, 0.0)
    sent = pltpu.make_async_copy(fine, fine_out, sems.at[10])
    sent.start()
    saved.wait()
    sent.wait()


def turn(x):
    n = x.shape[0] // 8
    x = x.reshape(n, 8, 128)
    row = lax.broadcasted_iota(jnp.int32, (n, 8, 128), 1)
    group = lax.broadcasted_iota(jnp.int32, (n, 8, 128), 2) // 16
    for d in (1, 2, 4):
        up = pltpu.roll(pltpu.roll(x, 8 - d, 1), 16 * d, 2)
        down = pltpu.roll(pltpu.roll(x, d, 1), 128 - 16 * d, 2)
        rb, gb = row & d, group & d
        x = jnp.where(rb == gb, x, jnp.where(rb == 0, up, down))
    return x.reshape(n * 8, 128)


def pack_coarse_kernel(
    rate_in, source_in, coarse_in, weighted_in, pick_in, octs_in, mean_in, out_hbm,
    rate, source, coarse, weighted, pick, octs, mean, out, turned, planes, table, mr, sems,
):
    copies = begin(
        sems,
        [(pick_in, pick)]
        + [(coarse_in.at[:, lo : lo + 7], coarse.at[:, lo : lo + 7]) for lo in range(0, S, 7)]
        + [(octs_in, octs), (mean_in, mean), (weighted_in, weighted), (rate_in, rate), (source_in, source)],
    )
    copies[0].wait()
    sel = pick[...]
    for i, lo in enumerate(range(0, S, 7)):
        copies[1 + i].wait()
        got = dot(coarse[0, lo : lo + 7].reshape(224, AREA), sel)
        for t in range(2):
            for s in range(7):
                turned[t, (lo + s) * 32 : (lo + s + 1) * 32, :] = turn(got[s * 32 : s * 32 + 32, 128 * t : 128 * t + 128])
    for c in copies[4:]:
        c.wait()
    planes[...] = jnp.zeros_like(planes)
    for w, p in enumerate((0, 15, 16, 31)):
        for s in range(S):
            planes[w * SLOTS + s : w * SLOTS + s + 1, :] = coarse[0, s, p : p + 1, :]
    for o in range(8):
        table[o, 12 * S :, :] = jnp.zeros((256 - 12 * S, 128), F32)
    for oy in range(2):
        for k2 in range(2):
            c = oy * 2 + k2
            got = dot(planes[:, 256 * c : 256 * c + 256], octs[...])
            for w in range(4):
                for oz in range(2):
                    o, fk = 4 * (w // 2) + 2 * oy + oz, (w % 2) * 2 + k2
                    table[o, fk * S : (fk + 1) * S, :] = got[w * SLOTS : w * SLOTS + S, oz * 128 : oz * 128 + 128]
    for t in range(2):
        for g in range(4):
            ox, k2 = g // 2, g % 2
            for w in range(4):
                for i in range(2):
                    oy, oz = (w // 2, i) if t == 0 else (i, w // 2)
                    f = 2 + 2 * t + w % 2
                    fk = f * 2 + k2
                    table[4 * ox + 2 * oy + oz, fk * S : (fk + 1) * S, :] = turned[
                        t, pl.ds(g * 8 + w * 2 + i, S, stride=32), :
                    ]
    row = lax.broadcasted_iota(jnp.int32, (SLOTS, 128), 0)
    rates = jnp.zeros((SLOTS, 128), F32)
    for s in range(S):
        rates = jnp.where(row == slot(s), rate[s], rates)
    averaged = dot(weighted[...], mean[...])
    mr[12 * S :, :] = jnp.zeros((256 - 12 * S, 128), F32)
    for fk in range(12):
        v = averaged[fk * SLOTS : (fk + 1) * SLOTS] * (rates * jnp.where(source[0, fk // 2] < 0, 1.0, 0.0))
        mr[fk * S : fk * S + HALF, :] = v[:HALF]
        mr[fk * S + HALF : (fk + 1) * S, :] = v[ROWS : ROWS + S - HALF]
    for j in range(PIECES):
        for o in range(8):
            out[j, o * CROWS : (o + 1) * CROWS, :] = table[o, j * CROWS : (j + 1) * CROWS, :]
        out[j, 8 * CROWS :, :] = mr[j * CROWS : (j + 1) * CROWS, :]
    sent = pltpu.make_async_copy(out, out_hbm, sems.at[9])
    sent.start()
    sent.wait()


def inner_kernel(rate, state, conduct, react, out, coef):
    kap = conduct[0]
    up = (lax.broadcasted_iota(jnp.int32, (S * 8, S), 0) // 8 == lax.broadcasted_iota(jnp.int32, (S * 8, S), 1)).astype(BF16)
    across = (lax.broadcasted_iota(jnp.int32, (S, S * 8), 1) // 8 == lax.broadcasted_iota(jnp.int32, (S, S * 8), 0)).astype(BF16)
    wide = (S * 8, S * 8)
    same = lax.broadcasted_iota(jnp.int32, wide, 0) % 8 == lax.broadcasted_iota(jnp.int32, wide, 1) % 8
    high = react[...].astype(BF16)
    low = (react[...] - high.astype(F32)).astype(BF16)

    def widened(r):
        tall = jnp.dot(up, r, preferred_element_type=F32).astype(BF16)
        return jnp.where(same, jnp.dot(tall, across, preferred_element_type=F32), 0.0).astype(BF16)

    react_hi, react_lo = widened(high), widened(low)
    col = lax.broadcasted_iota(jnp.int32, (B, AREA), 1)
    row = lax.broadcasted_iota(jnp.int32, (B, AREA), 0)
    y, z = col // 32, col % 32
    diag = jnp.zeros((B, AREA), F32)
    for i, (axis, step, at, end) in enumerate(
        ((0, 1, row, 0), (0, B - 1, row, 31), (1, 32, y, 0), (1, AREA - 32, y, 31), (1, 1, z, 0), (1, AREA - 1, z, 31))
    ):
        edge = at == end
        c = 0.5 * (kap + pltpu.roll(kap, step, axis))
        diag = diag + jnp.where(edge, kap, c)
        coef[i] = jnp.where(edge, 0.0, c)
    coef[6] = diag
    for g in range(4):
        x = state[0, :, g * 8 : g * 8 + 8, :].reshape(S * 8, AREA)
        hi = x.astype(BF16)
        lo = (x - hi.astype(F32)).astype(BF16)
        got = jnp.dot(react_hi, hi, preferred_element_type=F32)
        got += jnp.dot(react_hi, lo, preferred_element_type=F32)
        got += jnp.dot(react_lo, hi, preferred_element_type=F32)
        out[0, :, g * 8 : g * 8 + 8, :] = got.reshape(S, 8, AREA)

    def species(s, carry):
        u = state[0, s]
        acc = -coef[6] * u
        for i, (axis, step) in enumerate(((0, 1), (0, B - 1), (1, 32), (1, AREA - 32), (1, 1), (1, AREA - 1))):
            acc = acc + coef[i] * pltpu.roll(u, step, axis)
        out[0, s] = out[0, s] + rate[s] * acc
        return carry

    lax.fori_loop(0, S, species, 0)


def relay_kernel(note, rate, before, own, after, got, out, table):
    j = lax.axis_index("node")
    at = lax.broadcasted_iota(jnp.int32, (CROWS, 128), 0) + CROWS * j
    species = at % S
    first = at // S == (CROWS * j) // S
    rates = jnp.zeros((CROWS, 128), F32)
    for s in range(S):
        rates = jnp.where(species == s, rate[s], rates)
    out[:, FINE + CROWS :, :] = jnp.zeros((PIECES, 8 * CROWS, 128), F32)
    for n in range(PIECES):
        p = note[n, 6]
        c, o = p // 8, (p % 8) * CROWS
        piece = got[c, pl.ds(pl.multiple_of(o, CROWS), CROWS), :]
        out[n, FINE : FINE + CROWS, :] = piece
        kap = jnp.where(first, own[n, 23:24, :], own[n, 35:36, :])
        flux = got[n, 8 * CROWS :, :] - kap * rates * piece
        here = pl.ds(pl.multiple_of(o + FINE + CROWS, 8), CROWS)
        out[c, here, :] = out[c, here, :] + flux
    for g, ref in enumerate((before, own, after)):
        for n in range(PIECES):
            for f in range(6):
                table[g * 96 + n * 6 + f, :ROWS, :] = ref[n, f * ROWS : (f + 1) * ROWS, :]
    for n in range(PIECES):
        for f in range(6):
            q = jnp.maximum(note[n, f], 0)
            out[n, f * ROWS : (f + 1) * ROWS, :] = table[q, :ROWS, :]


def outer_kernel(
    rate, source, got, inner_in, conduct_in, spread_in, place_in, out_hbm, reg_hbm,
    inner, conduct, spread, place, out, reg, crow, cslot, wide, xs, edge, table, sems,
):
    copies = begin(
        sems,
        [(spread_in, spread), (place_in, place), (conduct_in, conduct)]
        + [(inner_in.at[:, lo:hi], inner.at[:, lo:hi]) for lo, hi in CHUNKS],
    )
    for j in range(PIECES):
        crow[j * CROWS : (j + 1) * CROWS, :] = got[j, FINE : FINE + CROWS, :]
        for o in range(8):
            at = FINE + CROWS + o * CROWS
            table[o * 256 + j * CROWS : o * 256 + (j + 1) * CROWS, :] = got[j, at : at + CROWS, :]
    for s in range(S):
        for k2 in range(2):
            for o in range(8):
                reg[0, s, o * 6 : o * 6 + 6, k2 * 128 : k2 * 128 + 128] = table[
                    pl.ds(o * 256 + k2 * S + s, 6, stride=2 * S), :
                ]
    kept = pltpu.make_async_copy(reg, reg_hbm, sems.at[7])
    kept.start()
    copies[0].wait()
    cslot[...] = jnp.zeros_like(cslot)
    for fk in range(12):
        cslot[fk * SLOTS : fk * SLOTS + HALF, :] = crow[fk * S : fk * S + HALF, :]
        cslot[fk * SLOTS + ROWS : fk * SLOTS + ROWS + S - HALF, :] = crow[fk * S + HALF : (fk + 1) * S, :]
    wide[...] = dot(cslot[...], spread[...])
    for k in range(8):
        k2, kk = k // 4, k % 4
        slabs = []
        for f in range(6):
            fine = jnp.concatenate(
                [got[2 * k, f * ROWS : (f + 1) * ROWS, :], got[2 * k + 1, f * ROWS : (f + 1) * ROWS, :]], 0
            )
            at = (f * 2 + k2) * SLOTS
            slabs.append(jnp.where(source[0, f] >= 0, fine, wide[at : at + SLOTS, 128 * kk : 128 * kk + 128]))
        for side in range(2):
            xs[side, :, 128 * k : 128 * k + 128] = slabs[side]
        for q, v in enumerate(swap_blocks(slabs[2:])):
            edge[pl.ds(4 * k + q, SLOTS, stride=32), :] = v
    copies[1].wait()
    copies[2].wait()
    kap = conduct[0]
    row = lax.broadcasted_iota(jnp.int32, (B, AREA), 0)
    done = []
    for i, (lo, hi) in enumerate(CHUNKS):
        ghost = dot(edge[slot(lo) * 32 : (slot(lo) + hi - lo) * 32, :], place[...])
        copies[3 + i].wait()
        for s in range(lo, hi):
            mine = ghost[(s - lo) * 32 : (s - lo + 1) * 32]
            mine = mine + jnp.where(row == 0, xs[0, slot(s) : slot(s) + 1, :], 0.0)
            mine = mine + jnp.where(row == 31, xs[1, slot(s) : slot(s) + 1, :], 0.0)
            out[0, s] = inner[0, s] + rate[s] * (kap * mine)
        c = pltpu.make_async_copy(out.at[:, lo:hi], out_hbm.at[:, lo:hi], sems.at[8 + i])
        c.start()
        done.append(c)
    kept.wait()
    for c in done:
        c.wait()


SPECS = {
    "v": pl.BlockSpec(memory_space=pltpu.VMEM),
    "s": pl.BlockSpec(memory_space=pltpu.SMEM),
    "a": pl.BlockSpec(memory_space=pl.ANY),
}


def call(kernel, ins, outs, spec, scratch, args, limit, copies=0, flops=int(1e9)):
    shapes = [jax.ShapeDtypeStruct(o, F32) for o in outs]
    moved = sum(a.size * a.dtype.itemsize for a in args) + sum(4 * int(np.prod(o)) for o in outs)
    scratch = [x if not isinstance(x, tuple) else pltpu.VMEM(x, F32) for x in scratch]
    return pl.pallas_call(
        kernel,
        out_shape=shapes if len(outs) > 1 else shapes[0],
        in_specs=[SPECS[c] for c in ins],
        out_specs=[SPECS[spec]] * len(outs) if len(outs) > 1 else SPECS[spec],
        scratch_shapes=scratch + ([pltpu.SemaphoreType.DMA((copies,))] if copies else []),
        compiler_params=pltpu.CompilerParams(vmem_limit_bytes=limit << 20),
        cost_estimate=pl.CostEstimate(flops=flops, bytes_accessed=moved, transcendentals=0),
        name=kernel.__name__.removesuffix("_kernel"),
    )(*args)


def shifted(block, distance):
    devices = range(lax.axis_size("sfc"))
    return lax.ppermute(block, "sfc", [(i, i + distance) for i in devices if i + distance in devices])


def exchange(block):
    return lax.all_to_all(block, "node", 0, 0, tiled=True)


def local(fine_state, conduct, spec_rate, reaction, coarse_state, ghost_source, parent_box):
    pick = jnp.asarray(pick_fine(), BF16)
    place = jnp.asarray(pick_fine().T, BF16)
    mean = jnp.asarray(average(), BF16)
    spread = jnp.asarray(4 * average().T, BF16)
    box = (1, S, B, AREA)
    fine, weighted = call(
        pack_fine_kernel,
        "aaaaaa",
        [(PIECES, FINE, 128), (12 * SLOTS, 512)],
        "a",
        [
            pltpu.SMEM((1, 6), jnp.int32), pltpu.SMEM((1,), jnp.int32), box, (1, B, AREA),
            pltpu.VMEM((AREA, 128), BF16), pltpu.VMEM((512, 128), BF16), (PIECES, FINE, 128), (12 * SLOTS, 512),
            (SLOTS * 32, 128), (2, SLOTS, AREA), (16, 512),
        ],
        (ghost_source, parent_box, fine_state, conduct, pick, mean),
        58,
        11,
    )
    own = exchange(fine)
    coarse = call(
        pack_coarse_kernel,
        "aaaaaaa",
        [(PIECES, 9 * CROWS, 128)],
        "a",
        [
            pltpu.SMEM((S,), F32), pltpu.SMEM((1, 6), jnp.int32), box, (12 * SLOTS, 512),
            pltpu.VMEM((AREA, 256), BF16), pltpu.VMEM((256, 256), BF16), pltpu.VMEM((512, 128), BF16),
            (PIECES, 9 * CROWS, 128), (2, S * 32, 128), (4 * SLOTS, AREA), (8, 256, 128), (256, 128),
        ],
        (spec_rate, ghost_source, coarse_state, weighted, jnp.asarray(pick_coarse(), BF16), jnp.asarray(split_octants(), BF16), mean),
        58,
        10,
    )
    grouped = exchange(coarse)
    before, after = shifted(own, 1), shifted(own, -1)
    inner = call(inner_kernel, "svvv", [box], "v", [(7, B, AREA)], (spec_rate, fine_state, conduct, reaction), 24)
    note = own[:, 11, :8].astype(jnp.int32)
    before, inner = lax.optimization_barrier((before, inner))
    chosen = call(
        relay_kernel,
        "ssvvvv",
        [(PIECES, FINE + 9 * CROWS, 128)],
        "v",
        [(3 * 96, ROWS, 128)],
        (note, spec_rate, before, own, after, grouped),
        24,
    )
    mine = exchange(chosen)
    tendency, register = call(
        outer_kernel,
        "ssvaaaa",
        [box, (1, S, 48, 256)],
        "a",
        [
            box, (1, B, AREA), pltpu.VMEM((128, 512), BF16), pltpu.VMEM((128, AREA), BF16), box, (1, S, 48, 256),
            (256, 128), (12 * SLOTS, 128), (12 * SLOTS, 512), (2, SLOTS, AREA), (SLOTS * 32, 128), (8 * 256, 128),
        ],
        (spec_rate, ghost_source, mine, inner, conduct, spread, place),
        32,
        12,
    )
    return tendency, register.transpose(0, 2, 1, 3)


def solution(mesh):
    box = P(("sfc", "node"))
    return jax.shard_map(
        local,
        mesh=mesh,
        in_specs=(box, box, P(), P(), box, box, box),
        out_specs=(box, box),
        check_vma=False,
    )
```

```python
import functools

import jax
import jax.numpy as jnp
import numpy as np
from jax import lax
from jax.experimental import pallas as pl
from jax.experimental.pallas import tpu as pltpu
from jax.sharding import PartitionSpec as P

S, B, AREA = 21, 32, 1024
PIECES = 16
HALF = 11
SLOTS = 24
ROWS = 12
FINE = 6 * ROWS
PART = 3
FACE = 48
CAP = 16
LIST = CAP * PART
MEANS = 24
F32, BF16 = jnp.float32, jnp.bfloat16


def slot(s):
    return s if s < HALF else s + 1


def pick_fine():
    m = np.zeros((AREA, 128), np.float32)
    for b in range(32):
        m[b, b] = 1
        m[31 * 32 + b, 32 + b] = 1
        m[b * 32, 64 + b] = 1
        m[b * 32 + 31, 96 + b] = 1
    return m


def pick_coarse():
    m = np.zeros((AREA, 256), np.float32)
    for w, p in enumerate((0, 15, 16, 31)):
        for b in range(32):
            m[p * 32 + b, w * 32 + b] = 1
            m[b * 32 + p, 128 + w * 32 + b] = 1
    return m


def split_octants():
    m = np.zeros((256, 256), np.float32)
    for a in range(8):
        for o in range(2):
            for b in range(16):
                m[a * 32 + o * 16 + b, o * 128 + a * 16 + b] = 1
    return m


def average():
    m = np.zeros((512, 128), np.float32)
    for a in range(16):
        for b in range(32):
            m[a * 32 + b, (a // 2) * 16 + b // 2] = 0.25
    return m


def dot(x, m):
    hi = x.astype(BF16)
    lo = (x - hi.astype(F32)).astype(BF16)
    return jnp.dot(hi, m, preferred_element_type=F32) + jnp.dot(lo, m, preferred_element_type=F32)


def dot_twice(x, m):
    hi = x.astype(BF16)
    lo = (x - hi.astype(F32)).astype(BF16)
    return jnp.dot(jnp.concatenate([hi, lo], 1), m, preferred_element_type=F32)


def lanes(rows):
    return lax.broadcasted_iota(jnp.int32, (rows, 128), 1)


def swap_blocks(parts):
    block = lanes(parts[0].shape[0]) // 32
    out = []
    for f in range(4):
        acc = None
        for q in range(4):
            moved = parts[q] if q == f else pltpu.roll(parts[q], (32 * (q - f)) % 128, 1)
            acc = moved if acc is None else jnp.where(block == q, moved, acc)
        out.append(acc)
    return out


CHUNKS = ((0, 6), (6, 11), (11, 16), (16, 21))


def begin(sems, pairs):
    copies = [pltpu.make_async_copy(src, dst, sems.at[i]) for i, (src, dst) in enumerate(pairs)]
    for c in copies:
        c.start()
    return copies


def pack_fine_kernel(
    source_in, parent_in, state_in, conduct_in, pick_in, fine_out, weighted_out,
    source, parent, state, conduct, pick, fine, weighted, edge, xs, sems,
):
    copies = begin(
        sems,
        [(pick_in, pick), (conduct_in, conduct)]
        + [(state_in.at[:, lo:hi], state.at[:, lo:hi]) for lo, hi in CHUNKS]
        + [(source_in, source), (parent_in, parent)],
    )
    edge[HALF * 32 : HALF * 32 + 32, :] = jnp.zeros((32, 128), F32)
    edge[22 * 32 : 23 * 32, :] = jnp.zeros((32, 128), F32)
    for side in range(2):
        for r in (11, 22):
            xs[side, r : r + 1, :] = jnp.zeros((1, AREA), F32)
    copies[0].wait()
    copies[1].wait()
    sel = pick[...]
    edge[23 * 32 : 24 * 32, :] = dot(conduct[0], sel)
    xs[0, 23:24, :] = conduct[0, 0:1, :]
    xs[1, 23:24, :] = conduct[0, 31:32, :]
    for i, (lo, hi) in enumerate(CHUNKS):
        copies[2 + i].wait()
        got = dot(state[0, lo:hi].reshape((hi - lo) * 32, AREA), sel)
        edge[slot(lo) * 32 : (slot(lo) + hi - lo) * 32, :] = got
        for s in range(lo, hi):
            xs[0, slot(s) : slot(s) + 1, :] = state[0, s, 0:1, :]
            xs[1, slot(s) : slot(s) + 1, :] = state[0, s, 31:32, :]
    row = lax.broadcasted_iota(jnp.int32, (SLOTS, 128), 0)
    for c in copies[6:]:
        c.wait()
    lane = lanes(1)
    note = jnp.where(lane == 6, parent[0], 0)
    for f in range(6):
        note = jnp.where(lane == f, source[0, f], note)
    note = note.astype(F32)
    sent = []
    for k in range(8):
        across = [xs[side, :, 128 * k : 128 * k + 128] for side in range(2)]
        across += swap_blocks([edge[pl.ds(4 * k + q, SLOTS, stride=32), :] for q in range(4)])
        k2, kk = k // 4, k % 4
        for f in range(6):
            t = across[f]
            fine[2 * k, f * ROWS : (f + 1) * ROWS, :] = t[:ROWS]
            fine[2 * k + 1, f * ROWS : (f + 1) * ROWS, :] = t[ROWS:]
            at = f * 2 + k2
            kap = jnp.broadcast_to(t[23:24], (SLOTS, 128))
            weighted[at * SLOTS : (at + 1) * SLOTS, 128 * kk : 128 * kk + 128] = jnp.where(row == 23, t, t * kap)
        for j in (2 * k, 2 * k + 1):
            fine[j, 11:12, :] = note
        c = pltpu.make_async_copy(fine.at[2 * k : 2 * k + 2], fine_out.at[2 * k : 2 * k + 2], sems.at[8 + k])
        c.start()
        sent.append(c)
    c = pltpu.make_async_copy(weighted, weighted_out, sems.at[16])
    c.start()
    for c in sent + [c]:
        c.wait()


def turn(x):
    n = x.shape[0] // 8
    x = x.reshape(n, 8, 128)
    row = lax.broadcasted_iota(jnp.int32, (n, 8, 128), 1)
    group = lax.broadcasted_iota(jnp.int32, (n, 8, 128), 2) // 16
    for d in (1, 2, 4):
        up = pltpu.roll(pltpu.roll(x, 8 - d, 1), 16 * d, 2)
        down = pltpu.roll(pltpu.roll(x, d, 1), 128 - 16 * d, 2)
        rb, gb = row & d, group & d
        x = jnp.where(rb == gb, x, jnp.where(rb == 0, up, down))
    return x.reshape(n * 8, 128)


def pack_coarse_kernel(
    rate_in, source_in, coarse_in, weighted_in, pick_in, octs_in, mean_in, packed_out, first_out, second_out,
    rate, source, coarse, weighted, pick, octs, mean, turned, planes, packed, first, second, sems,
):
    copies = begin(
        sems,
        [(pick_in, pick)]
        + [(coarse_in.at[:, lo : lo + 7], coarse.at[:, lo : lo + 7]) for lo in range(0, S, 7)]
        + [(octs_in, octs), (mean_in, mean), (weighted_in, weighted), (rate_in, rate), (source_in, source)],
    )
    copies[0].wait()
    sel = pick[...]
    for i, lo in enumerate(range(0, S, 7)):
        copies[1 + i].wait()
        got = dot(coarse[0, lo : lo + 7].reshape(224, AREA), sel)
        for t in range(2):
            for s in range(7):
                turned[t, (lo + s) * 32 : (lo + s + 1) * 32, :] = turn(got[s * 32 : s * 32 + 32, 128 * t : 128 * t + 128])
    for c in copies[4:]:
        c.wait()
    planes[...] = jnp.zeros_like(planes)
    for w, p in enumerate((0, 15, 16, 31)):
        for s in range(S):
            planes[w * SLOTS + s : w * SLOTS + s + 1, :] = coarse[0, s, p : p + 1, :]
    for at in range(48):
        packed[at * FACE + 2 * S : (at + 1) * FACE, :] = jnp.zeros((FACE - 2 * S, 128), F32)
    for oy in range(2):
        for k2 in range(2):
            c = oy * 2 + k2
            got = dot(planes[:, 256 * c : 256 * c + 256], octs[...])
            for w in range(4):
                for oz in range(2):
                    at = (4 * (w // 2) + 2 * oy + oz) * 6 + w % 2
                    at = at * FACE + k2 * S
                    packed[at : at + S, :] = got[w * SLOTS : w * SLOTS + S, oz * 128 : oz * 128 + 128]
    for t in range(2):
        for g in range(4):
            ox, k2 = g // 2, g % 2
            for w in range(4):
                for i in range(2):
                    oy, oz = (w // 2, i) if t == 0 else (i, w // 2)
                    f = 2 + 2 * t + w % 2
                    at = ((4 * ox + 2 * oy + oz) * 6 + f) * FACE + k2 * S
                    packed[at : at + S, :] = turned[
                        t, pl.ds(g * 8 + w * 2 + i, S, stride=32), :
                    ]
    saved = []
    row = lax.broadcasted_iota(jnp.int32, (SLOTS, 128), 0)
    rates = jnp.zeros((SLOTS, 128), F32)
    for s in range(S):
        rates = jnp.where(row == slot(s), rate[s], rates)
    averaged = dot(weighted[...], mean[...])
    for f in range(6):
        keep = jnp.where(source[0, f] < 0, 1.0, 0.0)
        for ref in (first, second):
            ref[f, 2 * S :, :] = jnp.zeros((FACE - 2 * S, 128), F32)
        for k2 in range(2):
            v = averaged[(f * 2 + k2) * SLOTS : (f * 2 + k2 + 1) * SLOTS] * keep
            kap = v[23:24]
            for ref, w in ((first, v * rates), (second, jnp.broadcast_to(kap, (SLOTS, 128)) * rates)):
                ref[f, k2 * S : k2 * S + HALF, :] = w[:HALF]
                ref[f, k2 * S + HALF : (k2 + 1) * S, :] = w[ROWS : ROWS + S - HALF]
            for j in range(7 * k2, 7 * k2 + (7 if k2 == 0 else 9)):
                at = 48 * FACE + j * MEANS + 18 + f
                packed[at : at + 1, :] = kap
        for j in range(PIECES):
            at = 48 * FACE + j * MEANS + PART * f
            packed[at : at + PART, :] = first[f, PART * j : PART * j + PART, :]
    for i, (src, dst) in enumerate(((packed, packed_out), (first, first_out), (second, second_out))):
        c = pltpu.make_async_copy(src, dst, sems.at[9 + i])
        c.start()
        saved.append(c)
    for c in saved:
        c.wait()


def choose_kernel(note, packed, out_hbm, mine, out, count, sems):
    me = lax.axis_index("node")
    count[0] = 0
    for n in range(PIECES):
        p = note[n, 6]

        @pl.when(p // 8 == me)
        def _(n=n, p=p):
            at = count[0]
            for f in range(6):
                hit = note[n, f] < 0
                mine[jnp.where(hit, jnp.minimum(at, CAP), CAP)] = (p % 8) * 6 + f
                at = at + hit.astype(jnp.int32)
            count[0] = at

    for i in range(CAP):
        mine[i] = jnp.where(i < count[0], mine[i], 48)
        face = packed[pl.ds(pl.multiple_of(jnp.minimum(mine[i], 47) * FACE, 8), FACE), :]
        for j in range(PIECES):
            out[j, PART * i : PART * i + PART, :] = face[PART * j : PART * j + PART]
    for j in range(PIECES):
        out[j, LIST:, :] = packed[48 * FACE + j * MEANS : 48 * FACE + (j + 1) * MEANS, :]
    sent = pltpu.make_async_copy(out, out_hbm, sems.at[0])
    sent.start()
    sent.wait()


def inner_kernel(rate, state, conduct, react, later, out, coef):
    del later
    kap = conduct[0]
    up = (lax.broadcasted_iota(jnp.int32, (S * 8, S), 0) // 8 == lax.broadcasted_iota(jnp.int32, (S * 8, S), 1)).astype(BF16)
    across = (lax.broadcasted_iota(jnp.int32, (S, S * 8), 1) // 8 == lax.broadcasted_iota(jnp.int32, (S, S * 8), 0)).astype(BF16)
    wide = (S * 8, S * 8)
    same = lax.broadcasted_iota(jnp.int32, wide, 0) % 8 == lax.broadcasted_iota(jnp.int32, wide, 1) % 8
    high = react[...].astype(BF16)
    low = (react[...] - high.astype(F32)).astype(BF16)

    def widened(r):
        tall = jnp.dot(up, r, preferred_element_type=F32).astype(BF16)
        return jnp.where(same, jnp.dot(tall, across, preferred_element_type=F32), 0.0).astype(BF16)

    react_hi, react_lo = widened(high), widened(low)
    col = lax.broadcasted_iota(jnp.int32, (B, AREA), 1)
    row = lax.broadcasted_iota(jnp.int32, (B, AREA), 0)
    y, z = col // 32, col % 32
    diag = jnp.zeros((B, AREA), F32)
    for i, (axis, step, at, end) in enumerate(
        ((0, 1, row, 0), (0, B - 1, row, 31), (1, 32, y, 0), (1, AREA - 32, y, 31), (1, 1, z, 0), (1, AREA - 1, z, 31))
    ):
        edge = at == end
        c = 0.5 * (kap + pltpu.roll(kap, step, axis))
        diag = diag + jnp.where(edge, kap, c)
        coef[i] = jnp.where(edge, 0.0, c)
    coef[6] = diag
    for g in range(4):
        x = state[0, :, g * 8 : g * 8 + 8, :].reshape(S * 8, AREA)
        hi = x.astype(BF16)
        lo = (x - hi.astype(F32)).astype(BF16)
        got = jnp.dot(react_hi, hi, preferred_element_type=F32)
        got += jnp.dot(react_hi, lo, preferred_element_type=F32)
        got += jnp.dot(react_lo, hi, preferred_element_type=F32)
        out[0, :, g * 8 : g * 8 + 8, :] = got.reshape(S, 8, AREA)

    def species(s, carry):
        u = state[0, s]
        acc = -coef[6] * u
        for i, (axis, step) in enumerate(((0, 1), (0, B - 1), (1, 32), (1, AREA - 32), (1, 1), (1, AREA - 1))):
            acc = acc + coef[i] * pltpu.roll(u, step, axis)
        out[0, s] = out[0, s] + rate[s] * acc
        return carry

    lax.fori_loop(0, S, species, 0)


def relay_kernel(note, rate, before, own, after, got, out_hbm, over, out, table, listed, fluxes, seen, sems):
    for c in range(PIECES):
        seen[c] = 0
    j = lax.axis_index("node")
    species = (lax.broadcasted_iota(jnp.int32, (PART, 128), 0) + PART * j) % S
    rates = jnp.zeros((PART, 128), F32)
    for s in range(S):
        rates = jnp.where(species == s, rate[s], rates)
    for c in range(PIECES):
        for i in range(CAP):
            listed[c * CAP + i, :PART, :] = got[c, PART * i : PART * i + PART, :]
    for g, ref in enumerate((before, own, after)):
        for n in range(PIECES):
            for f in range(6):
                table[g * 96 + n * 6 + f, :ROWS, :] = ref[n, f * ROWS : (f + 1) * ROWS, :]
    for n in range(PIECES):
        c = note[n, 6] // 8
        place = seen[c]
        for f in range(6):
            q = note[n, f]
            rank = jnp.where(q < 0, jnp.minimum(place, CAP), CAP)
            place = jnp.where(q < 0, place + 1, place)
            fine = table[jnp.maximum(q, 0), :ROWS, :]
            e = c * CAP + jnp.minimum(rank, CAP - 1)
            piece = listed[e, :PART, :]
            out[n, f * ROWS + PART : (f + 1) * ROWS, :] = fine[PART:]
            out[n, f * ROWS : f * ROWS + PART, :] = jnp.where(q >= 0, fine[:PART], piece)
            kap = got[n, LIST + 18 + f : LIST + 19 + f, :]
            flux = got[n, LIST + PART * f : LIST + PART * f + PART, :] - kap * rates * piece
            fluxes[jnp.where(rank < CAP, e, PIECES * CAP), :PART, :] = flux
        seen[c] = place
    most = seen[0]
    for c in range(1, PIECES):
        most = jnp.maximum(most, seen[c])
    over[0] = (most > CAP).astype(jnp.int32)
    for c in range(PIECES):
        for i in range(CAP):
            out[c, FINE + PART * i : FINE + PART * i + PART, :] = fluxes[c * CAP + i, :PART, :]
    sent = pltpu.make_async_copy(out, out_hbm, sems.at[0])
    sent.start()
    sent.wait()


def outer_kernel(
    rate, source, listed, over, got, inner_in, conduct_in, spread_in, place_in, ghost_in, rows_in, out_hbm, reg_hbm,
    inner, conduct, spread, place, out, reg, crow, cslot, wide, xs, edge, table, held, sems,
):
    copies = begin(
        sems,
        [(spread_in, spread), (place_in, place), (conduct_in, conduct)]
        + [(inner_in.at[:, lo:hi], inner.at[:, lo:hi]) for lo, hi in CHUNKS],
    )
    table[...] = jnp.zeros_like(table)
    for i in range(CAP):
        held[i, 2 * S :, :] = jnp.zeros((FACE - 2 * S, 128), F32)
    for j in range(14):
        at = slice(PART * j, PART * j + PART)
        for f in range(6):
            crow[f, at, :] = got[j, f * ROWS : f * ROWS + PART, :]
        for i in range(CAP):
            held[i, at, :] = got[j, FINE + PART * i : FINE + PART * i + PART, :]
    for i in range(CAP):
        face = pl.ds(pl.multiple_of(listed[i] * FACE, 8), FACE)
        table[face, :] = table[face, :] + held[i]

    @pl.when(over[0] > 0)
    def _():
        for src, dst, sem in ((ghost_in, crow, sems.at[12]), (rows_in, table.at[: 48 * FACE], sems.at[13])):
            c = pltpu.make_async_copy(src, dst, sem)
            c.start()
            c.wait()

    for s in range(S):
        for k2 in range(2):
            reg[0, s, :, k2 * 128 : k2 * 128 + 128] = table[pl.ds(k2 * S + s, 48, stride=FACE), :]
    kept = pltpu.make_async_copy(reg, reg_hbm, sems.at[7])
    kept.start()
    copies[0].wait()
    cslot[...] = jnp.zeros_like(cslot)
    for fk in range(12):
        at = fk % 2 * S
        cslot[fk * SLOTS : fk * SLOTS + HALF, :] = crow[fk // 2, at : at + HALF, :]
        cslot[fk * SLOTS + ROWS : fk * SLOTS + ROWS + S - HALF, :] = crow[fk // 2, at + HALF : at + S, :]
    wide[...] = dot_twice(cslot[...], spread[...])
    for k in range(8):
        k2, kk = k // 4, k % 4
        slabs = []
        for f in range(6):
            fine = jnp.concatenate(
                [got[2 * k, f * ROWS : (f + 1) * ROWS, :], got[2 * k + 1, f * ROWS : (f + 1) * ROWS, :]], 0
            )
            at = (f * 2 + k2) * SLOTS
            slabs.append(jnp.where(source[0, f] >= 0, fine, wide[at : at + SLOTS, 128 * kk : 128 * kk + 128]))
        for side in range(2):
            xs[side, :, 128 * k : 128 * k + 128] = slabs[side]
        for q, v in enumerate(swap_blocks(slabs[2:])):
            edge[pl.ds(4 * k + q, SLOTS, stride=32), :] = v
    copies[1].wait()
    copies[2].wait()
    kap = conduct[0]
    for side in range(2):
        xs[side] = xs[side] * kap[31 * side : 31 * side + 1]
    done = []
    for i, (lo, hi) in enumerate(CHUNKS):
        ghost = dot_twice(edge[slot(lo) * 32 : (slot(lo) + hi - lo) * 32, :], place[...])
        copies[3 + i].wait()
        for s in range(lo, hi):
            out[0, s] = inner[0, s] + rate[s] * (kap * ghost[(s - lo) * 32 : (s - lo + 1) * 32])
            for side in range(2):
                at = slice(31 * side, 31 * side + 1)
                out[0, s, at, :] = out[0, s, at, :] + rate[s] * xs[side, slot(s) : slot(s) + 1, :]
        c = pltpu.make_async_copy(out.at[:, lo:hi], out_hbm.at[:, lo:hi], sems.at[8 + i])
        c.start()
        done.append(c)
    kept.wait()
    for c in done:
        c.wait()


SPECS = {
    "v": pl.BlockSpec(memory_space=pltpu.VMEM),
    "s": pl.BlockSpec(memory_space=pltpu.SMEM),
    "a": pl.BlockSpec(memory_space=pl.ANY),
}


def call(kernel, ins, outs, spec, scratch, args, limit, copies=0, flops=int(1e9), alias={}):
    shapes = [jax.ShapeDtypeStruct(o, jnp.int32 if c == "s" else F32) for o, c in zip(outs, spec)]
    moved = sum(a.size * a.dtype.itemsize for a in args) + sum(4 * int(np.prod(o)) for o in outs)
    scratch = [x if not isinstance(x, tuple) else pltpu.VMEM(x, F32) for x in scratch]
    return pl.pallas_call(
        kernel,
        out_shape=shapes if len(outs) > 1 else shapes[0],
        in_specs=[SPECS[c] for c in ins],
        out_specs=[SPECS[c] for c in spec] if len(outs) > 1 else SPECS[spec],
        scratch_shapes=scratch + ([pltpu.SemaphoreType.DMA((copies,))] if copies else []),
        input_output_aliases=alias,
        compiler_params=pltpu.CompilerParams(vmem_limit_bytes=limit << 20),
        cost_estimate=pl.CostEstimate(flops=flops, bytes_accessed=moved, transcendentals=0),
        name=kernel.__name__.removesuffix("_kernel"),
    )(*args)


def shifted(block, distance):
    devices = range(lax.axis_size("sfc"))
    return lax.ppermute(block, "sfc", [(i, i + distance) for i in devices if i + distance in devices])


def exchange(block):
    return lax.all_to_all(block, "node", 0, 0, tiled=True)


def gathered(note, packed, first, second):
    me = lax.axis_index("node")
    parents = note[:, 6]
    parent = parents[me]
    ring = [(i, (i + 1) % PIECES) for i in range(PIECES)]
    size = 6 * FACE

    def faces_step(i, held):
        faces, ghost = held
        owner = (me - i) % PIECES
        mine = lax.dynamic_slice(faces, (parent % 8 * size, 0), (size, 128))
        ghost = jnp.where(parent // 8 == owner, mine, ghost)
        return lax.ppermute(faces, "node", ring), ghost

    _, ghost = lax.fori_loop(0, PIECES, faces_step, (packed[: 8 * size], jnp.zeros((size, 128), F32)))

    def flux_step(i, held):
        flux, rows = held
        box = (me - i) % PIECES
        at = (parents[box] % 8 * size, 0)
        added = lax.dynamic_slice(rows, at, (size, 128)) + flux
        return lax.ppermute(flux, "node", ring), jnp.where(parents[box] // 8 == me, lax.dynamic_update_slice(rows, added, at), rows)

    flux = first.reshape(size, 128) - second.reshape(size, 128) * ghost
    _, rows = lax.fori_loop(0, PIECES, flux_step, (flux, jnp.zeros((8 * size, 128), F32)))
    return ghost.reshape(6, FACE, 128), rows


def local(fine_state, conduct, spec_rate, reaction, coarse_state, ghost_source, parent_box):
    pick = jnp.asarray(pick_fine(), BF16)
    place = jnp.asarray(np.tile(pick_fine().T, (2, 1)), BF16)
    mean = jnp.asarray(average(), BF16)
    spread = jnp.asarray(np.tile(4 * average().T, (2, 1)), BF16)
    box = (1, S, B, AREA)
    fine, weighted = call(
        pack_fine_kernel,
        "aaaaa",
        [(PIECES, FINE, 128), (12 * SLOTS, 512)],
        "aa",
        [
            pltpu.SMEM((1, 6), jnp.int32), pltpu.SMEM((1,), jnp.int32), box, (1, B, AREA),
            pltpu.VMEM((AREA, 128), BF16), (PIECES, FINE, 128), (12 * SLOTS, 512), (SLOTS * 32, 128), (2, SLOTS, AREA),
        ],
        (ghost_source, parent_box, fine_state, conduct, pick),
        58,
        17,
    )
    own = exchange(fine)
    packed, first, second = call(
        pack_coarse_kernel,
        "aaaaaaa",
        [(48 * FACE + PIECES * MEANS, 128), (6, FACE, 128), (6, FACE, 128)],
        "aaa",
        [
            pltpu.SMEM((S,), F32), pltpu.SMEM((1, 6), jnp.int32), box, (12 * SLOTS, 512),
            pltpu.VMEM((AREA, 256), BF16), pltpu.VMEM((256, 256), BF16), pltpu.VMEM((512, 128), BF16),
            (2, S * 32, 128), (4 * SLOTS, AREA), (48 * FACE + PIECES * MEANS, 128), (6, FACE, 128), (6, FACE, 128),
        ],
        (spec_rate, ghost_source, coarse_state, weighted, jnp.asarray(pick_coarse(), BF16), jnp.asarray(split_octants(), BF16), mean),
        58,
        13,
    )
    note = own[:, 11, :8].astype(jnp.int32)
    coarse, listed = call(
        choose_kernel,
        "sv",
        [(PIECES, LIST + MEANS, 128), (CAP + 1,)],
        "as",
        [(PIECES, LIST + MEANS, 128), pltpu.SMEM((1,), jnp.int32)],
        (note, packed),
        24,
        1,
    )
    before, after = shifted(own, 1), shifted(own, -1)
    grouped = exchange(coarse)
    chosen, over = call(
        relay_kernel,
        "ssvvvv",
        [(PIECES, FINE + LIST, 128), (1,)],
        "as",
        [
            (PIECES, FINE + LIST, 128), (3 * 96, ROWS, 128), (PIECES * CAP, PART, 128), (PIECES * CAP + 1, PART, 128),
            pltpu.SMEM((PIECES,), jnp.int32),
        ],
        (note, spec_rate, before, own, after, grouped),
        24,
        1,
    )
    mine = exchange(chosen)
    inner = call(inner_kernel, "svvva", [box], "v", [(7, B, AREA)], (spec_rate, fine_state, conduct, reaction, chosen), 24)
    ghost, rows = lax.cond(
        over[0] > 0,
        gathered,
        lambda note, packed, first, second: (first, packed[: 48 * FACE]),
        note, packed, first, second,
    )
    tendency, register = call(
        outer_kernel,
        "ssssvaaaaaa",
        [box, (1, S, 48, 256)],
        "aa",
        [
            box, (1, B, AREA), pltpu.VMEM((256, 512), BF16), pltpu.VMEM((256, AREA), BF16), box, (1, S, 48, 256),
            (6, FACE, 128), (12 * SLOTS, 128), (12 * SLOTS, 512), (2, SLOTS, AREA), (SLOTS * 32, 128), (49 * FACE, 128), (CAP, FACE, 128),
        ],
        (spec_rate, ghost_source, listed, over, mine, inner, conduct, spread, place, ghost, rows),
        58,
        14,
    )
    return tendency, register.transpose(0, 2, 1, 3)


def solution(mesh):
    box = P(("sfc", "node"))
    return jax.shard_map(
        local,
        mesh=mesh,
        in_specs=(box, box, P(), P(), box, box, box),
        out_specs=(box, box),
        check_vma=False,
    )
```

```python
import functools

import jax
import jax.numpy as jnp
import numpy as np
from jax import lax
from jax.experimental import pallas as pl
from jax.experimental.pallas import tpu as pltpu
from jax.sharding import PartitionSpec as P

S, B, AREA = 21, 32, 1024
PIECES = 16
HALF = 11
SLOTS = 24
ROWS = 12
FINE = 6 * ROWS
PART = 3
FACE = 48
CAP = 16
LIST = CAP * PART
MEANS = 24
F32, BF16 = jnp.float32, jnp.bfloat16


def slot(s):
    return s if s < HALF else s + 1


def pick_fine():
    m = np.zeros((AREA, 128), np.float32)
    for b in range(32):
        m[b, b] = 1
        m[31 * 32 + b, 32 + b] = 1
        m[b * 32, 64 + b] = 1
        m[b * 32 + 31, 96 + b] = 1
    return m


def pick_coarse():
    m = np.zeros((AREA, 256), np.float32)
    for w, p in enumerate((0, 15, 16, 31)):
        for b in range(32):
            m[p * 32 + b, w * 32 + b] = 1
            m[b * 32 + p, 128 + w * 32 + b] = 1
    return m


def split_octants():
    m = np.zeros((256, 256), np.float32)
    for a in range(8):
        for o in range(2):
            for b in range(16):
                m[a * 32 + o * 16 + b, o * 128 + a * 16 + b] = 1
    return m


def average():
    m = np.zeros((512, 128), np.float32)
    for a in range(16):
        for b in range(32):
            m[a * 32 + b, (a // 2) * 16 + b // 2] = 0.25
    return m


def dot(x, m):
    hi = x.astype(BF16)
    lo = (x - hi.astype(F32)).astype(BF16)
    return jnp.dot(hi, m, preferred_element_type=F32) + jnp.dot(lo, m, preferred_element_type=F32)


def dot_twice(x, m):
    hi = x.astype(BF16)
    lo = (x - hi.astype(F32)).astype(BF16)
    return jnp.dot(jnp.concatenate([hi, lo], 1), m, preferred_element_type=F32)


def lanes(rows):
    return lax.broadcasted_iota(jnp.int32, (rows, 128), 1)


def swap_blocks(parts):
    block = lanes(parts[0].shape[0]) // 32
    out = []
    for f in range(4):
        acc = None
        for q in range(4):
            moved = parts[q] if q == f else pltpu.roll(parts[q], (32 * (q - f)) % 128, 1)
            acc = moved if acc is None else jnp.where(block == q, moved, acc)
        out.append(acc)
    return out


CHUNKS = ((0, 6), (6, 11), (11, 16), (16, 21))


def begin(sems, pairs):
    copies = [pltpu.make_async_copy(src, dst, sems.at[i]) for i, (src, dst) in enumerate(pairs)]
    for c in copies:
        c.start()
    return copies


def pack_fine_kernel(
    source_in, parent_in, state_in, conduct_in, pick_in, fine_out, weighted_out,
    source, parent, state, conduct, pick, fine, weighted, edge, xs, sems,
):
    copies = begin(
        sems,
        [(pick_in, pick), (conduct_in, conduct)]
        + [(state_in.at[:, lo:hi], state.at[:, lo:hi]) for lo, hi in CHUNKS]
        + [(source_in, source), (parent_in, parent)],
    )
    edge[HALF * 32 : HALF * 32 + 32, :] = jnp.zeros((32, 128), F32)
    edge[22 * 32 : 23 * 32, :] = jnp.zeros((32, 128), F32)
    for side in range(2):
        for r in (11, 22):
            xs[side, r : r + 1, :] = jnp.zeros((1, AREA), F32)
    copies[0].wait()
    copies[1].wait()
    sel = pick[...]
    edge[23 * 32 : 24 * 32, :] = dot(conduct[0], sel)
    xs[0, 23:24, :] = conduct[0, 0:1, :]
    xs[1, 23:24, :] = conduct[0, 31:32, :]
    for i, (lo, hi) in enumerate(CHUNKS):
        copies[2 + i].wait()
        got = dot(state[0, lo:hi].reshape((hi - lo) * 32, AREA), sel)
        edge[slot(lo) * 32 : (slot(lo) + hi - lo) * 32, :] = got
        for s in range(lo, hi):
            xs[0, slot(s) : slot(s) + 1, :] = state[0, s, 0:1, :]
            xs[1, slot(s) : slot(s) + 1, :] = state[0, s, 31:32, :]
    row = lax.broadcasted_iota(jnp.int32, (SLOTS, 128), 0)
    for c in copies[6:]:
        c.wait()
    lane = lanes(1)
    note = jnp.where(lane == 6, parent[0], 0)
    for f in range(6):
        note = jnp.where(lane == f, source[0, f], note)
    note = note.astype(F32)
    sent = []
    for k in range(8):
        across = [xs[side, :, 128 * k : 128 * k + 128] for side in range(2)]
        across += swap_blocks([edge[pl.ds(4 * k + q, SLOTS, stride=32), :] for q in range(4)])
        k2, kk = k // 4, k % 4
        for f in range(6):
            t = across[f]
            fine[2 * k, f * ROWS : (f + 1) * ROWS, :] = t[:ROWS]
            fine[2 * k + 1, f * ROWS : (f + 1) * ROWS, :] = t[ROWS:]
            at = f * 2 + k2
            kap = jnp.broadcast_to(t[23:24], (SLOTS, 128))
            weighted[at * SLOTS : (at + 1) * SLOTS, 128 * kk : 128 * kk + 128] = jnp.where(row == 23, t, t * kap)
        for j in (2 * k, 2 * k + 1):
            fine[j, 11:12, :] = note
        c = pltpu.make_async_copy(fine.at[2 * k : 2 * k + 2], fine_out.at[2 * k : 2 * k + 2], sems.at[8 + k])
        c.start()
        sent.append(c)
    c = pltpu.make_async_copy(weighted, weighted_out, sems.at[16])
    c.start()
    for c in sent + [c]:
        c.wait()


def turn(x):
    n = x.shape[0] // 8
    x = x.reshape(n, 8, 128)
    row = lax.broadcasted_iota(jnp.int32, (n, 8, 128), 1)
    group = lax.broadcasted_iota(jnp.int32, (n, 8, 128), 2) // 16
    for d in (1, 2, 4):
        up = pltpu.roll(pltpu.roll(x, 8 - d, 1), 16 * d, 2)
        down = pltpu.roll(pltpu.roll(x, d, 1), 128 - 16 * d, 2)
        rb, gb = row & d, group & d
        x = jnp.where(rb == gb, x, jnp.where(rb == 0, up, down))
    return x.reshape(n * 8, 128)


def pack_coarse_kernel(
    rate_in, source_in, coarse_in, weighted_in, pick_in, octs_in, mean_in, packed_out, first_out, second_out,
    rate, source, coarse, weighted, pick, octs, mean, turned, planes, packed, first, second, sems,
):
    copies = begin(
        sems,
        [(pick_in, pick)]
        + [(coarse_in.at[:, lo : lo + 7], coarse.at[:, lo : lo + 7]) for lo in range(0, S, 7)]
        + [(octs_in, octs), (mean_in, mean), (weighted_in, weighted), (rate_in, rate), (source_in, source)],
    )
    copies[0].wait()
    sel = pick[...]
    for i, lo in enumerate(range(0, S, 7)):
        copies[1 + i].wait()
        got = dot(coarse[0, lo : lo + 7].reshape(224, AREA), sel)
        for t in range(2):
            for s in range(7):
                turned[t, (lo + s) * 32 : (lo + s + 1) * 32, :] = turn(got[s * 32 : s * 32 + 32, 128 * t : 128 * t + 128])
    for c in copies[4:]:
        c.wait()
    planes[...] = jnp.zeros_like(planes)
    for w, p in enumerate((0, 15, 16, 31)):
        for s in range(S):
            planes[w * SLOTS + s : w * SLOTS + s + 1, :] = coarse[0, s, p : p + 1, :]
    for at in range(48):
        packed[at * FACE + 2 * S : (at + 1) * FACE, :] = jnp.zeros((FACE - 2 * S, 128), F32)
    for oy in range(2):
        for k2 in range(2):
            c = oy * 2 + k2
            got = dot(planes[:, 256 * c : 256 * c + 256], octs[...])
            for w in range(4):
                for oz in range(2):
                    at = (4 * (w // 2) + 2 * oy + oz) * 6 + w % 2
                    at = at * FACE + k2 * S
                    packed[at : at + S, :] = got[w * SLOTS : w * SLOTS + S, oz * 128 : oz * 128 + 128]
    for t in range(2):
        for g in range(4):
            ox, k2 = g // 2, g % 2
            for w in range(4):
                for i in range(2):
                    oy, oz = (w // 2, i) if t == 0 else (i, w // 2)
                    f = 2 + 2 * t + w % 2
                    at = ((4 * ox + 2 * oy + oz) * 6 + f) * FACE + k2 * S
                    packed[at : at + S, :] = turned[
                        t, pl.ds(g * 8 + w * 2 + i, S, stride=32), :
                    ]
    saved = []
    row = lax.broadcasted_iota(jnp.int32, (SLOTS, 128), 0)
    rates = jnp.zeros((SLOTS, 128), F32)
    for s in range(S):
        rates = jnp.where(row == slot(s), rate[s], rates)
    averaged = dot(weighted[...], mean[...])
    for f in range(6):
        keep = jnp.where(source[0, f] < 0, 1.0, 0.0)
        for ref in (first, second):
            ref[f, 2 * S :, :] = jnp.zeros((FACE - 2 * S, 128), F32)
        for k2 in range(2):
            v = averaged[(f * 2 + k2) * SLOTS : (f * 2 + k2 + 1) * SLOTS] * keep
            kap = v[23:24]
            for ref, w in ((first, v * rates), (second, jnp.broadcast_to(kap, (SLOTS, 128)) * rates)):
                ref[f, k2 * S : k2 * S + HALF, :] = w[:HALF]
                ref[f, k2 * S + HALF : (k2 + 1) * S, :] = w[ROWS : ROWS + S - HALF]
            for j in range(7 * k2, 7 * k2 + (7 if k2 == 0 else 9)):
                at = 48 * FACE + j * MEANS + 18 + f
                packed[at : at + 1, :] = kap
        for j in range(PIECES):
            at = 48 * FACE + j * MEANS + PART * f
            packed[at : at + PART, :] = first[f, PART * j : PART * j + PART, :]
    for i, (src, dst) in enumerate(((packed, packed_out), (first, first_out), (second, second_out))):
        c = pltpu.make_async_copy(src, dst, sems.at[9 + i])
        c.start()
        saved.append(c)
    for c in saved:
        c.wait()


def choose_kernel(note, packed, out_hbm, mine, out, count, sems):
    me = lax.axis_index("node")
    count[0] = 0
    for n in range(PIECES):
        p = note[n, 6]

        @pl.when(p // 8 == me)
        def _(n=n, p=p):
            at = count[0]
            for f in range(6):
                hit = note[n, f] < 0
                mine[jnp.where(hit, jnp.minimum(at, CAP), CAP)] = (p % 8) * 6 + f
                at = at + hit.astype(jnp.int32)
            count[0] = at

    for i in range(CAP):
        mine[i] = jnp.where(i < count[0], mine[i], 48)
        face = packed[pl.ds(pl.multiple_of(jnp.minimum(mine[i], 47) * FACE, 8), FACE), :]
        for j in range(PIECES):
            out[j, PART * i : PART * i + PART, :] = face[PART * j : PART * j + PART]
    for j in range(PIECES):
        out[j, LIST:, :] = packed[48 * FACE + j * MEANS : 48 * FACE + (j + 1) * MEANS, :]
    sent = pltpu.make_async_copy(out, out_hbm, sems.at[0])
    sent.start()
    sent.wait()


def inner_kernel(rate, state, conduct, react, later, out, coef):
    del later
    kap = conduct[0]
    up = (lax.broadcasted_iota(jnp.int32, (S * 8, S), 0) // 8 == lax.broadcasted_iota(jnp.int32, (S * 8, S), 1)).astype(BF16)
    across = (lax.broadcasted_iota(jnp.int32, (S, S * 8), 1) // 8 == lax.broadcasted_iota(jnp.int32, (S, S * 8), 0)).astype(BF16)
    wide = (S * 8, S * 8)
    same = lax.broadcasted_iota(jnp.int32, wide, 0) % 8 == lax.broadcasted_iota(jnp.int32, wide, 1) % 8
    high = react[...].astype(BF16)
    low = (react[...] - high.astype(F32)).astype(BF16)

    def widened(r):
        tall = jnp.dot(up, r, preferred_element_type=F32).astype(BF16)
        return jnp.where(same, jnp.dot(tall, across, preferred_element_type=F32), 0.0).astype(BF16)

    react_hi, react_lo = widened(high), widened(low)
    col = lax.broadcasted_iota(jnp.int32, (B, AREA), 1)
    row = lax.broadcasted_iota(jnp.int32, (B, AREA), 0)
    y, z = col // 32, col % 32
    diag = jnp.zeros((B, AREA), F32)
    for i, (axis, step, at, end) in enumerate(
        ((0, 1, row, 0), (0, B - 1, row, 31), (1, 32, y, 0), (1, AREA - 32, y, 31), (1, 1, z, 0), (1, AREA - 1, z, 31))
    ):
        edge = at == end
        c = 0.5 * (kap + pltpu.roll(kap, step, axis))
        diag = diag + jnp.where(edge, kap, c)
        coef[i] = jnp.where(edge, 0.0, c)
    coef[6] = diag
    for g in range(4):
        x = state[0, :, g * 8 : g * 8 + 8, :].reshape(S * 8, AREA)
        hi = x.astype(BF16)
        lo = (x - hi.astype(F32)).astype(BF16)
        got = jnp.dot(react_hi, hi, preferred_element_type=F32)
        got += jnp.dot(react_hi, lo, preferred_element_type=F32)
        got += jnp.dot(react_lo, hi, preferred_element_type=F32)
        out[0, :S, g * 8 : g * 8 + 8, :] = got.reshape(S, 8, AREA)

    out[0, S] = kap
    def species(s, carry):
        u = state[0, s]
        acc = -coef[6] * u
        for i, (axis, step) in enumerate(((0, 1), (0, B - 1), (1, 32), (1, AREA - 32), (1, 1), (1, AREA - 1))):
            acc = acc + coef[i] * pltpu.roll(u, step, axis)
        out[0, s] = out[0, s] + rate[s] * acc
        return carry

    lax.fori_loop(0, S, species, 0)


def relay_kernel(note, chosen, rate, before, own, after, got, out_hbm, plan, out, table, listed, fluxes, seen, sems):
    for c in range(PIECES):
        seen[c] = 0
    j = lax.axis_index("node")
    species = (lax.broadcasted_iota(jnp.int32, (PART, 128), 0) + PART * j) % S
    rates = jnp.zeros((PART, 128), F32)
    for s in range(S):
        rates = jnp.where(species == s, rate[s], rates)
    for c in range(PIECES):
        for i in range(CAP):
            listed[c * CAP + i, :PART, :] = got[c, PART * i : PART * i + PART, :]
    for g, ref in enumerate((before, own, after)):
        for n in range(PIECES):
            for f in range(6):
                table[g * 96 + n * 6 + f, :ROWS, :] = ref[n, f * ROWS : (f + 1) * ROWS, :]
    for n in range(PIECES):
        c = note[n, 6] // 8
        place = seen[c]
        for f in range(6):
            q = note[n, f]
            rank = jnp.where(q < 0, jnp.minimum(place, CAP), CAP)
            place = jnp.where(q < 0, place + 1, place)
            fine = table[jnp.maximum(q, 0), :ROWS, :]
            e = c * CAP + jnp.minimum(rank, CAP - 1)
            piece = listed[e, :PART, :]
            out[n, f * ROWS + PART : (f + 1) * ROWS, :] = fine[PART:]
            out[n, f * ROWS : f * ROWS + PART, :] = jnp.where(q >= 0, fine[:PART], piece)
            kap = got[n, LIST + 18 + f : LIST + 19 + f, :]
            flux = got[n, LIST + PART * f : LIST + PART * f + PART, :] - kap * rates * piece
            fluxes[jnp.where(rank < CAP, e, PIECES * CAP), :PART, :] = flux
        seen[c] = place
    most = seen[0]
    for c in range(1, PIECES):
        most = jnp.maximum(most, seen[c])
    plan[0] = (most > CAP).astype(jnp.int32)
    for i in range(CAP):
        plan[1 + i] = chosen[i]
    for f in range(6):
        plan[1 + CAP + f] = note[j, f]
    slots = pltpu.make_async_copy(out.at[:, :FINE], out_hbm.at[:, :FINE], sems.at[0])
    slots.start()
    for c in range(PIECES):
        for i in range(CAP):
            out[c, FINE + PART * i : FINE + PART * i + PART, :] = fluxes[c * CAP + i, :PART, :]
    sent = pltpu.make_async_copy(out.at[:, FINE:], out_hbm.at[:, FINE:], sems.at[1])
    sent.start()
    slots.wait()
    sent.wait()


def spread_matrix():
    r = lax.broadcasted_iota(jnp.int32, (256, 512), 0) % 128
    c = lax.broadcasted_iota(jnp.int32, (256, 512), 1)
    return jnp.logical_and(r // 16 == c // 64, r % 16 == c % 32 // 2).astype(F32).astype(BF16)


def place_matrix():
    r = lax.broadcasted_iota(jnp.int32, (256, AREA), 0) % 128
    c = lax.broadcasted_iota(jnp.int32, (256, AREA), 1)
    y, z, f, b = c // 32, c % 32, r // 32, r % 32
    at, along = jnp.where(f < 2, y, z), jnp.where(f < 2, z, y)
    return jnp.logical_and(at == (f % 2) * 31, along == b).astype(F32).astype(BF16)


def outer_kernel(
    rate, plan, got, inner, ghost_in, rows_in, out_hbm, reg_hbm,
    out, reg, crow, cslot, wide, xs, edge, table, held, sems,
):
    table[...] = jnp.zeros_like(table)
    for i in range(CAP):
        held[i, 2 * S :, :] = jnp.zeros((FACE - 2 * S, 128), F32)
    for j in range(14):
        at = slice(PART * j, PART * j + PART)
        for f in range(6):
            crow[f, at, :] = got[j, f * ROWS : f * ROWS + PART, :]
        for i in range(CAP):
            held[i, at, :] = got[j, FINE + PART * i : FINE + PART * i + PART, :]
    for i in range(CAP):
        face = pl.ds(pl.multiple_of(plan[1 + i] * FACE, 8), FACE)
        table[face, :] = table[face, :] + held[i]

    @pl.when(plan[0] > 0)
    def _():
        for src, dst, sem in ((ghost_in, crow, sems.at[12]), (rows_in, table.at[: 48 * FACE], sems.at[13])):
            c = pltpu.make_async_copy(src, dst, sem)
            c.start()
            c.wait()

    for s in range(S):
        for k2 in range(2):
            reg[0, s, :, k2 * 128 : k2 * 128 + 128] = table[pl.ds(k2 * S + s, 48, stride=FACE), :]
    kept = pltpu.make_async_copy(reg, reg_hbm, sems.at[7])
    kept.start()
    cslot[...] = jnp.zeros_like(cslot)
    for fk in range(12):
        at = fk % 2 * S
        cslot[fk * SLOTS : fk * SLOTS + HALF, :] = crow[fk // 2, at : at + HALF, :]
        cslot[fk * SLOTS + ROWS : fk * SLOTS + ROWS + S - HALF, :] = crow[fk // 2, at + HALF : at + S, :]
    wide[...] = dot_twice(cslot[...], spread_matrix())
    for k in range(8):
        k2, kk = k // 4, k % 4
        slabs = []
        for f in range(6):
            fine = jnp.concatenate(
                [got[2 * k, f * ROWS : (f + 1) * ROWS, :], got[2 * k + 1, f * ROWS : (f + 1) * ROWS, :]], 0
            )
            at = (f * 2 + k2) * SLOTS
            slabs.append(jnp.where(plan[1 + CAP + f] >= 0, fine, wide[at : at + SLOTS, 128 * kk : 128 * kk + 128]))
        for side in range(2):
            xs[side, :, 128 * k : 128 * k + 128] = slabs[side]
        for q, v in enumerate(swap_blocks(slabs[2:])):
            edge[pl.ds(4 * k + q, SLOTS, stride=32), :] = v
    kap = inner[0, S]
    place = place_matrix()
    for side in range(2):
        xs[side] = xs[side] * kap[31 * side : 31 * side + 1]
    done = []
    for i, (lo, hi) in enumerate(CHUNKS):
        ghost = dot_twice(edge[slot(lo) * 32 : (slot(lo) + hi - lo) * 32, :], place)
        for s in range(lo, hi):
            out[0, s] = inner[0, s] + rate[s] * (kap * ghost[(s - lo) * 32 : (s - lo + 1) * 32])
            for side in range(2):
                at = slice(31 * side, 31 * side + 1)
                out[0, s, at, :] = out[0, s, at, :] + rate[s] * xs[side, slot(s) : slot(s) + 1, :]
        c = pltpu.make_async_copy(out.at[:, lo:hi], out_hbm.at[:, lo:hi], sems.at[8 + i])
        c.start()
        done.append(c)
    kept.wait()
    for c in done:
        c.wait()


SPECS = {
    "v": pl.BlockSpec(memory_space=pltpu.VMEM),
    "s": pl.BlockSpec(memory_space=pltpu.SMEM),
    "a": pl.BlockSpec(memory_space=pl.ANY),
}


def call(kernel, ins, outs, spec, scratch, args, limit, copies=0, flops=int(1e9), alias={}):
    shapes = [jax.ShapeDtypeStruct(o, jnp.int32 if c == "s" else F32) for o, c in zip(outs, spec)]
    moved = sum(a.size * a.dtype.itemsize for a in args) + sum(4 * int(np.prod(o)) for o in outs)
    scratch = [x if not isinstance(x, tuple) else pltpu.VMEM(x, F32) for x in scratch]
    return pl.pallas_call(
        kernel,
        out_shape=shapes if len(outs) > 1 else shapes[0],
        in_specs=[SPECS[c] for c in ins],
        out_specs=[SPECS[c] for c in spec] if len(outs) > 1 else SPECS[spec],
        scratch_shapes=scratch + ([pltpu.SemaphoreType.DMA((copies,))] if copies else []),
        input_output_aliases=alias,
        compiler_params=pltpu.CompilerParams(vmem_limit_bytes=limit << 20),
        cost_estimate=pl.CostEstimate(flops=flops, bytes_accessed=moved, transcendentals=0),
        name=kernel.__name__.removesuffix("_kernel"),
    )(*args)


def shifted(block, distance):
    devices = range(lax.axis_size("sfc"))
    return lax.ppermute(block, "sfc", [(i, i + distance) for i in devices if i + distance in devices])


def exchange(block):
    return lax.all_to_all(block, "node", 0, 0, tiled=True)


def gathered(note, packed, first, second):
    me = lax.axis_index("node")
    parents = note[:, 6]
    parent = parents[me]
    ring = [(i, (i + 1) % PIECES) for i in range(PIECES)]
    size = 6 * FACE

    def faces_step(i, held):
        faces, ghost = held
        owner = (me - i) % PIECES
        mine = lax.dynamic_slice(faces, (parent % 8 * size, 0), (size, 128))
        ghost = jnp.where(parent // 8 == owner, mine, ghost)
        return lax.ppermute(faces, "node", ring), ghost

    _, ghost = lax.fori_loop(0, PIECES, faces_step, (packed[: 8 * size], jnp.zeros((size, 128), F32)))

    def flux_step(i, held):
        flux, rows = held
        box = (me - i) % PIECES
        at = (parents[box] % 8 * size, 0)
        added = lax.dynamic_slice(rows, at, (size, 128)) + flux
        return lax.ppermute(flux, "node", ring), jnp.where(parents[box] // 8 == me, lax.dynamic_update_slice(rows, added, at), rows)

    flux = first.reshape(size, 128) - second.reshape(size, 128) * ghost
    _, rows = lax.fori_loop(0, PIECES, flux_step, (flux, jnp.zeros((8 * size, 128), F32)))
    return ghost.reshape(6, FACE, 128), rows


def local(fine_state, conduct, spec_rate, reaction, coarse_state, ghost_source, parent_box):
    pick = jnp.asarray(pick_fine(), BF16)
    mean = jnp.asarray(average(), BF16)
    box = (1, S, B, AREA)
    fine, weighted = call(
        pack_fine_kernel,
        "aaaaa",
        [(PIECES, FINE, 128), (12 * SLOTS, 512)],
        "aa",
        [
            pltpu.SMEM((1, 6), jnp.int32), pltpu.SMEM((1,), jnp.int32), box, (1, B, AREA),
            pltpu.VMEM((AREA, 128), BF16), (PIECES, FINE, 128), (12 * SLOTS, 512), (SLOTS * 32, 128), (2, SLOTS, AREA),
        ],
        (ghost_source, parent_box, fine_state, conduct, pick),
        58,
        17,
    )
    own = exchange(fine)
    packed, first, second = call(
        pack_coarse_kernel,
        "aaaaaaa",
        [(48 * FACE + PIECES * MEANS, 128), (6, FACE, 128), (6, FACE, 128)],
        "aaa",
        [
            pltpu.SMEM((S,), F32), pltpu.SMEM((1, 6), jnp.int32), box, (12 * SLOTS, 512),
            pltpu.VMEM((AREA, 256), BF16), pltpu.VMEM((256, 256), BF16), pltpu.VMEM((512, 128), BF16),
            (2, S * 32, 128), (4 * SLOTS, AREA), (48 * FACE + PIECES * MEANS, 128), (6, FACE, 128), (6, FACE, 128),
        ],
        (spec_rate, ghost_source, coarse_state, weighted, jnp.asarray(pick_coarse(), BF16), jnp.asarray(split_octants(), BF16), mean),
        58,
        13,
    )
    note = own[:, 11, :8].astype(jnp.int32)
    coarse, listed = call(
        choose_kernel,
        "sv",
        [(PIECES, LIST + MEANS, 128), (CAP + 1,)],
        "as",
        [(PIECES, LIST + MEANS, 128), pltpu.SMEM((1,), jnp.int32)],
        (note, packed),
        24,
        1,
    )
    before, after = shifted(own, 1), shifted(own, -1)
    grouped = exchange(coarse)
    chosen, plan = call(
        relay_kernel,
        "sssvvvv",
        [(PIECES, FINE + LIST, 128), (1 + CAP + 6,)],
        "as",
        [
            (PIECES, FINE + LIST, 128), (3 * 96, ROWS, 128), (PIECES * CAP, PART, 128), (PIECES * CAP + 1, PART, 128),
            pltpu.SMEM((PIECES,), jnp.int32),
        ],
        (note, listed, spec_rate, before, own, after, grouped),
        24,
        2,
    )
    mine = exchange(chosen)
    inner = call(inner_kernel, "svvva", [(1, S + 1, B, AREA)], "v", [(7, B, AREA)], (spec_rate, fine_state, conduct, reaction, chosen), 24)
    ghost, rows = lax.cond(
        plan[0] > 0,
        gathered,
        lambda note, packed, first, second: (first, packed[: 48 * FACE]),
        note, packed, first, second,
    )
    tendency, register = call(
        outer_kernel,
        "ssvvaa",
        [box, (1, S, 48, 256)],
        "aa",
        [
            box, (1, S, 48, 256),
            (6, FACE, 128), (12 * SLOTS, 128), (12 * SLOTS, 512), (2, SLOTS, AREA), (SLOTS * 32, 128), (49 * FACE, 128), (CAP, FACE, 128),
        ],
        (spec_rate, plan, mine, inner, ghost, rows),
        28,
        14,
    )
    return tendency, register.transpose(0, 2, 1, 3)


def solution(mesh):
    box = P(("sfc", "node"))
    return jax.shard_map(
        local,
        mesh=mesh,
        in_specs=(box, box, P(), P(), box, box, box),
        out_specs=(box, box),
        check_vma=False,
    )
```

```python
import functools

import jax
import jax.numpy as jnp
import numpy as np
from jax import lax
from jax.experimental import pallas as pl
from jax.experimental.pallas import tpu as pltpu
from jax.sharding import PartitionSpec as P

S, B, AREA = 21, 32, 1024
PIECES = 16
HALF = 11
SLOTS = 24
ROWS = 12
FINE = 6 * ROWS
PART = 3
FACE = 48
CAP = 16
LIST = CAP * PART
MEANS = 24
F32, BF16 = jnp.float32, jnp.bfloat16


def slot(s):
    return s if s < HALF else s + 1


def pick_fine():
    m = np.zeros((AREA, 128), np.float32)
    for b in range(32):
        m[b, b] = 1
        m[31 * 32 + b, 32 + b] = 1
        m[b * 32, 64 + b] = 1
        m[b * 32 + 31, 96 + b] = 1
    return m


def pick_coarse():
    m = np.zeros((AREA, 256), np.float32)
    for w, p in enumerate((0, 15, 16, 31)):
        for b in range(32):
            m[p * 32 + b, w * 32 + b] = 1
            m[b * 32 + p, 128 + w * 32 + b] = 1
    return m


def split_octants():
    m = np.zeros((256, 256), np.float32)
    for a in range(8):
        for o in range(2):
            for b in range(16):
                m[a * 32 + o * 16 + b, o * 128 + a * 16 + b] = 1
    return m


def average():
    m = np.zeros((512, 128), np.float32)
    for a in range(16):
        for b in range(32):
            m[a * 32 + b, (a // 2) * 16 + b // 2] = 0.25
    return m


def dot(x, m):
    hi = x.astype(BF16)
    lo = (x - hi.astype(F32)).astype(BF16)
    return jnp.dot(hi, m, preferred_element_type=F32) + jnp.dot(lo, m, preferred_element_type=F32)


def dot_twice(x, m):
    hi = x.astype(BF16)
    lo = (x - hi.astype(F32)).astype(BF16)
    return jnp.dot(jnp.concatenate([hi, lo], 1), m, preferred_element_type=F32)


def lanes(rows):
    return lax.broadcasted_iota(jnp.int32, (rows, 128), 1)


def swap_blocks(parts):
    block = lanes(parts[0].shape[0]) // 32
    out = []
    for f in range(4):
        acc = None
        for q in range(4):
            moved = parts[q] if q == f else pltpu.roll(parts[q], (32 * (q - f)) % 128, 1)
            acc = moved if acc is None else jnp.where(block == q, moved, acc)
        out.append(acc)
    return out


CHUNKS = ((0, 6), (6, 11), (11, 16), (16, 21))


def begin(sems, pairs):
    copies = [pltpu.make_async_copy(src, dst, sems.at[i]) for i, (src, dst) in enumerate(pairs)]
    for c in copies:
        c.start()
    return copies


def pack_fine_kernel(
    source_in, parent_in, state_in, conduct_in, pick_in, fine_out, weighted_out,
    source, parent, state, conduct, pick, fine, weighted, edge, xs, sems,
):
    copies = begin(
        sems,
        [(pick_in, pick), (conduct_in, conduct)]
        + [(state_in.at[:, lo:hi], state.at[:, lo:hi]) for lo, hi in CHUNKS]
        + [(source_in, source), (parent_in, parent)],
    )
    edge[HALF * 32 : HALF * 32 + 32, :] = jnp.zeros((32, 128), F32)
    edge[22 * 32 : 23 * 32, :] = jnp.zeros((32, 128), F32)
    for side in range(2):
        for r in (11, 22):
            xs[side, r : r + 1, :] = jnp.zeros((1, AREA), F32)
    copies[0].wait()
    copies[1].wait()
    sel = pick[...]
    edge[23 * 32 : 24 * 32, :] = dot(conduct[0], sel)
    xs[0, 23:24, :] = conduct[0, 0:1, :]
    xs[1, 23:24, :] = conduct[0, 31:32, :]
    for i, (lo, hi) in enumerate(CHUNKS):
        copies[2 + i].wait()
        got = dot(state[0, lo:hi].reshape((hi - lo) * 32, AREA), sel)
        edge[slot(lo) * 32 : (slot(lo) + hi - lo) * 32, :] = got
        for s in range(lo, hi):
            xs[0, slot(s) : slot(s) + 1, :] = state[0, s, 0:1, :]
            xs[1, slot(s) : slot(s) + 1, :] = state[0, s, 31:32, :]
    row = lax.broadcasted_iota(jnp.int32, (SLOTS, 128), 0)
    for c in copies[6:]:
        c.wait()
    lane = lanes(1)
    note = jnp.where(lane == 6, parent[0], 0)
    for f in range(6):
        note = jnp.where(lane == f, source[0, f], note)
    note = note.astype(F32)
    sent = []
    for k in range(8):
        across = [xs[side, :, 128 * k : 128 * k + 128] for side in range(2)]
        across += swap_blocks([edge[pl.ds(4 * k + q, SLOTS, stride=32), :] for q in range(4)])
        k2, kk = k // 4, k % 4
        for f in range(6):
            t = across[f]
            fine[2 * k, f * ROWS : (f + 1) * ROWS, :] = t[:ROWS]
            fine[2 * k + 1, f * ROWS : (f + 1) * ROWS, :] = t[ROWS:]
            at = f * 2 + k2
            kap = jnp.broadcast_to(t[23:24], (SLOTS, 128))
            weighted[at * SLOTS : (at + 1) * SLOTS, 128 * kk : 128 * kk + 128] = jnp.where(row == 23, t, t * kap)
        for j in (2 * k, 2 * k + 1):
            fine[j, 11:12, :] = note
        c = pltpu.make_async_copy(fine.at[2 * k : 2 * k + 2], fine_out.at[2 * k : 2 * k + 2], sems.at[8 + k])
        c.start()
        sent.append(c)
    c = pltpu.make_async_copy(weighted, weighted_out, sems.at[16])
    c.start()
    for c in sent + [c]:
        c.wait()


def turn(x):
    n = x.shape[0] // 8
    x = x.reshape(n, 8, 128)
    row = lax.broadcasted_iota(jnp.int32, (n, 8, 128), 1)
    group = lax.broadcasted_iota(jnp.int32, (n, 8, 128), 2) // 16
    for d in (1, 2, 4):
        up = pltpu.roll(pltpu.roll(x, 8 - d, 1), 16 * d, 2)
        down = pltpu.roll(pltpu.roll(x, d, 1), 128 - 16 * d, 2)
        rb, gb = row & d, group & d
        x = jnp.where(rb == gb, x, jnp.where(rb == 0, up, down))
    return x.reshape(n * 8, 128)


def pack_coarse_kernel(
    rate_in, source_in, coarse_in, weighted_in, pick_in, octs_in, mean_in, packed_out, first_out, second_out,
    rate, source, coarse, weighted, pick, octs, mean, turned, planes, packed, first, second, sems,
):
    copies = begin(
        sems,
        [(pick_in, pick)]
        + [(coarse_in.at[:, lo : lo + 7], coarse.at[:, lo : lo + 7]) for lo in range(0, S, 7)]
        + [(octs_in, octs), (mean_in, mean), (weighted_in, weighted), (rate_in, rate), (source_in, source)],
    )
    copies[0].wait()
    sel = pick[...]
    for i, lo in enumerate(range(0, S, 7)):
        copies[1 + i].wait()
        got = dot(coarse[0, lo : lo + 7].reshape(224, AREA), sel)
        for t in range(2):
            for s in range(7):
                turned[t, (lo + s) * 32 : (lo + s + 1) * 32, :] = turn(got[s * 32 : s * 32 + 32, 128 * t : 128 * t + 128])
    for c in copies[4:]:
        c.wait()
    planes[...] = jnp.zeros_like(planes)
    for w, p in enumerate((0, 15, 16, 31)):
        for s in range(S):
            planes[w * SLOTS + s : w * SLOTS + s + 1, :] = coarse[0, s, p : p + 1, :]
    for at in range(48):
        packed[at * FACE + 2 * S : (at + 1) * FACE, :] = jnp.zeros((FACE - 2 * S, 128), F32)
    for oy in range(2):
        for k2 in range(2):
            c = oy * 2 + k2
            got = dot(planes[:, 256 * c : 256 * c + 256], octs[...])
            for w in range(4):
                for oz in range(2):
                    at = (4 * (w // 2) + 2 * oy + oz) * 6 + w % 2
                    at = at * FACE + k2 * S
                    packed[at : at + S, :] = got[w * SLOTS : w * SLOTS + S, oz * 128 : oz * 128 + 128]
    for t in range(2):
        for g in range(4):
            ox, k2 = g // 2, g % 2
            for w in range(4):
                for i in range(2):
                    oy, oz = (w // 2, i) if t == 0 else (i, w // 2)
                    f = 2 + 2 * t + w % 2
                    at = ((4 * ox + 2 * oy + oz) * 6 + f) * FACE + k2 * S
                    packed[at : at + S, :] = turned[
                        t, pl.ds(g * 8 + w * 2 + i, S, stride=32), :
                    ]
    saved = []
    row = lax.broadcasted_iota(jnp.int32, (SLOTS, 128), 0)
    rates = jnp.zeros((SLOTS, 128), F32)
    for s in range(S):
        rates = jnp.where(row == slot(s), rate[s], rates)
    averaged = dot(weighted[...], mean[...])
    for f in range(6):
        keep = jnp.where(source[0, f] < 0, 1.0, 0.0)
        for ref in (first, second):
            ref[f, 2 * S :, :] = jnp.zeros((FACE - 2 * S, 128), F32)
        for k2 in range(2):
            v = averaged[(f * 2 + k2) * SLOTS : (f * 2 + k2 + 1) * SLOTS] * keep
            kap = v[23:24]
            for ref, w in ((first, v * rates), (second, jnp.broadcast_to(kap, (SLOTS, 128)) * rates)):
                ref[f, k2 * S : k2 * S + HALF, :] = w[:HALF]
                ref[f, k2 * S + HALF : (k2 + 1) * S, :] = w[ROWS : ROWS + S - HALF]
            for j in range(7 * k2, 7 * k2 + (7 if k2 == 0 else 9)):
                at = 48 * FACE + j * MEANS + 18 + f
                packed[at : at + 1, :] = kap
        for j in range(PIECES):
            at = 48 * FACE + j * MEANS + PART * f
            packed[at : at + PART, :] = first[f, PART * j : PART * j + PART, :]
    for i, (src, dst) in enumerate(((packed, packed_out), (first, first_out), (second, second_out))):
        c = pltpu.make_async_copy(src, dst, sems.at[9 + i])
        c.start()
        saved.append(c)
    for c in saved:
        c.wait()


def choose_kernel(note, packed, out_hbm, mine, out, count, sems):
    me = lax.axis_index("node")
    count[0] = 0
    for n in range(PIECES):
        p = note[n, 6]

        @pl.when(p // 8 == me)
        def _(n=n, p=p):
            at = count[0]
            for f in range(6):
                hit = note[n, f] < 0
                mine[jnp.where(hit, jnp.minimum(at, CAP), CAP)] = (p % 8) * 6 + f
                at = at + hit.astype(jnp.int32)
            count[0] = at

    for i in range(CAP):
        mine[i] = jnp.where(i < count[0], mine[i], 48)
        face = packed[pl.ds(pl.multiple_of(jnp.minimum(mine[i], 47) * FACE, 8), FACE), :]
        for j in range(PIECES):
            out[j, PART * i : PART * i + PART, :] = face[PART * j : PART * j + PART]
    for j in range(PIECES):
        out[j, LIST:, :] = packed[48 * FACE + j * MEANS : 48 * FACE + (j + 1) * MEANS, :]
    sent = pltpu.make_async_copy(out, out_hbm, sems.at[0])
    sent.start()
    sent.wait()


def inner_kernel(rate, state, conduct, react, later, out, coef):
    del later
    kap = conduct[0]
    up = (lax.broadcasted_iota(jnp.int32, (S * 8, S), 0) // 8 == lax.broadcasted_iota(jnp.int32, (S * 8, S), 1)).astype(BF16)
    across = (lax.broadcasted_iota(jnp.int32, (S, S * 8), 1) // 8 == lax.broadcasted_iota(jnp.int32, (S, S * 8), 0)).astype(BF16)
    wide = (S * 8, S * 8)
    same = lax.broadcasted_iota(jnp.int32, wide, 0) % 8 == lax.broadcasted_iota(jnp.int32, wide, 1) % 8
    high = react[...].astype(BF16)
    low = (react[...] - high.astype(F32)).astype(BF16)

    def widened(r):
        tall = jnp.dot(up, r, preferred_element_type=F32).astype(BF16)
        return jnp.where(same, jnp.dot(tall, across, preferred_element_type=F32), 0.0).astype(BF16)

    react_hi, react_lo = widened(high), widened(low)
    col = lax.broadcasted_iota(jnp.int32, (B, AREA), 1)
    row = lax.broadcasted_iota(jnp.int32, (B, AREA), 0)
    y, z = col // 32, col % 32
    diag = jnp.zeros((B, AREA), F32)
    for i, (axis, step, at, end) in enumerate(
        ((0, 1, row, 0), (0, B - 1, row, 31), (1, 32, y, 0), (1, AREA - 32, y, 31), (1, 1, z, 0), (1, AREA - 1, z, 31))
    ):
        edge = at == end
        c = 0.5 * (kap + pltpu.roll(kap, step, axis))
        diag = diag + jnp.where(edge, kap, c)
        coef[i] = jnp.where(edge, 0.0, c)
    coef[6] = diag
    for g in range(4):
        x = state[0, :, g * 8 : g * 8 + 8, :].reshape(S * 8, AREA)
        hi = x.astype(BF16)
        lo = (x - hi.astype(F32)).astype(BF16)
        got = jnp.dot(react_hi, hi, preferred_element_type=F32)
        got += jnp.dot(react_hi, lo, preferred_element_type=F32)
        got += jnp.dot(react_lo, hi, preferred_element_type=F32)
        out[0, :S, g * 8 : g * 8 + 8, :] = got.reshape(S, 8, AREA)

    out[0, S] = kap
    def species(s, carry):
        u = state[0, s]
        acc = -coef[6] * u
        for i, (axis, step) in enumerate(((0, 1), (0, B - 1), (1, 32), (1, AREA - 32), (1, 1), (1, AREA - 1))):
            acc = acc + coef[i] * pltpu.roll(u, step, axis)
        out[0, s] = out[0, s] + rate[s] * acc
        return carry

    lax.fori_loop(0, S, species, 0)


def relay_kernel(note, chosen, rate, before, own, after, got, out_hbm, plan, out, table, listed, fluxes, seen, sems):
    for c in range(PIECES):
        seen[c] = 0
    j = lax.axis_index("node")
    species = (lax.broadcasted_iota(jnp.int32, (PART, 128), 0) + PART * j) % S
    rates = jnp.zeros((PART, 128), F32)
    for s in range(S):
        rates = jnp.where(species == s, rate[s], rates)
    for c in range(PIECES):
        for i in range(CAP):
            listed[c * CAP + i, :PART, :] = got[c, PART * i : PART * i + PART, :]
    for g, ref in enumerate((before, own, after)):
        for n in range(PIECES):
            for f in range(6):
                table[g * 96 + n * 6 + f, :ROWS, :] = ref[n, f * ROWS : (f + 1) * ROWS, :]
    for n in range(PIECES):
        c = note[n, 6] // 8
        place = seen[c]
        for f in range(6):
            q = note[n, f]
            rank = jnp.where(q < 0, jnp.minimum(place, CAP), CAP)
            place = jnp.where(q < 0, place + 1, place)
            fine = table[jnp.maximum(q, 0), :ROWS, :]
            e = c * CAP + jnp.minimum(rank, CAP - 1)
            piece = listed[e, :PART, :]
            out[n, f * ROWS + PART : (f + 1) * ROWS, :] = fine[PART:]
            out[n, f * ROWS : f * ROWS + PART, :] = jnp.where(q >= 0, fine[:PART], piece)
            kap = got[n, LIST + 18 + f : LIST + 19 + f, :]
            flux = got[n, LIST + PART * f : LIST + PART * f + PART, :] - kap * rates * piece
            fluxes[jnp.where(rank < CAP, e, PIECES * CAP), :PART, :] = flux
        seen[c] = place
    most = seen[0]
    for c in range(1, PIECES):
        most = jnp.maximum(most, seen[c])
    plan[0] = (most > CAP).astype(jnp.int32)
    for i in range(CAP):
        plan[1 + i] = chosen[i]
    for f in range(6):
        plan[1 + CAP + f] = note[j, f]
    slots = pltpu.make_async_copy(out.at[:, :FINE], out_hbm.at[:, :FINE], sems.at[0])
    slots.start()
    for c in range(PIECES):
        for i in range(CAP):
            out[c, FINE + PART * i : FINE + PART * i + PART, :] = fluxes[c * CAP + i, :PART, :]
    sent = pltpu.make_async_copy(out.at[:, FINE:], out_hbm.at[:, FINE:], sems.at[1])
    sent.start()
    slots.wait()
    sent.wait()


def spread_matrix():
    r = lax.broadcasted_iota(jnp.int32, (128, 512), 0)
    c = lax.broadcasted_iota(jnp.int32, (128, 512), 1)
    m = jnp.logical_and(r // 16 == c // 64, r % 16 == c % 32 // 2).astype(F32).astype(BF16)
    return jnp.concatenate([m, m], 0)


def place_matrix():
    r = lax.broadcasted_iota(jnp.int32, (128, AREA), 0)
    c = lax.broadcasted_iota(jnp.int32, (128, AREA), 1)
    y, z, f, b = c // 32, c % 32, r // 32, r % 32
    at, along = jnp.where(f < 2, y, z), jnp.where(f < 2, z, y)
    m = jnp.logical_and(at == (f % 2) * 31, along == b).astype(F32).astype(BF16)
    return jnp.concatenate([m, m], 0)


def outer_kernel(
    rate, plan, got, inner, ghost_in, rows_in, out_hbm, reg_hbm,
    out, reg, crow, cslot, wide, xs, edge, table, held, sems,
):
    table[...] = jnp.zeros_like(table)
    for i in range(CAP):
        held[i, 2 * S :, :] = jnp.zeros((FACE - 2 * S, 128), F32)
    for j in range(14):
        at = slice(PART * j, PART * j + PART)
        for f in range(6):
            crow[f, at, :] = got[j, f * ROWS : f * ROWS + PART, :]
        for i in range(CAP):
            held[i, at, :] = got[j, FINE + PART * i : FINE + PART * i + PART, :]
    for i in range(CAP):
        face = pl.ds(pl.multiple_of(plan[1 + i] * FACE, 8), FACE)
        table[face, :] = table[face, :] + held[i]

    @pl.when(plan[0] > 0)
    def _():
        for src, dst, sem in ((ghost_in, crow, sems.at[12]), (rows_in, table.at[: 48 * FACE], sems.at[13])):
            c = pltpu.make_async_copy(src, dst, sem)
            c.start()
            c.wait()

    for s in range(S):
        for k2 in range(2):
            reg[0, s, :, k2 * 128 : k2 * 128 + 128] = table[pl.ds(k2 * S + s, 48, stride=FACE), :]
    kept = pltpu.make_async_copy(reg, reg_hbm, sems.at[7])
    kept.start()
    cslot[...] = jnp.zeros_like(cslot)
    for fk in range(12):
        at = fk % 2 * S
        cslot[fk * SLOTS : fk * SLOTS + HALF, :] = crow[fk // 2, at : at + HALF, :]
        cslot[fk * SLOTS + ROWS : fk * SLOTS + ROWS + S - HALF, :] = crow[fk // 2, at + HALF : at + S, :]
    wide[...] = dot_twice(cslot[...], spread_matrix())
    for k in range(8):
        k2, kk = k // 4, k % 4
        slabs = []
        for f in range(6):
            fine = jnp.concatenate(
                [got[2 * k, f * ROWS : (f + 1) * ROWS, :], got[2 * k + 1, f * ROWS : (f + 1) * ROWS, :]], 0
            )
            at = (f * 2 + k2) * SLOTS
            slabs.append(jnp.where(plan[1 + CAP + f] >= 0, fine, wide[at : at + SLOTS, 128 * kk : 128 * kk + 128]))
        for side in range(2):
            xs[side, :, 128 * k : 128 * k + 128] = slabs[side]
        for q, v in enumerate(swap_blocks(slabs[2:])):
            edge[pl.ds(4 * k + q, SLOTS, stride=32), :] = v
    kap = inner[0, S]
    place = place_matrix()
    for side in range(2):
        xs[side] = xs[side] * kap[31 * side : 31 * side + 1]
    done = []
    for i, (lo, hi) in enumerate(CHUNKS):
        ghost = dot_twice(edge[slot(lo) * 32 : (slot(lo) + hi - lo) * 32, :], place)
        for s in range(lo, hi):
            out[0, s] = inner[0, s] + rate[s] * (kap * ghost[(s - lo) * 32 : (s - lo + 1) * 32])
            for side in range(2):
                at = slice(31 * side, 31 * side + 1)
                out[0, s, at, :] = out[0, s, at, :] + rate[s] * xs[side, slot(s) : slot(s) + 1, :]
        c = pltpu.make_async_copy(out.at[:, lo:hi], out_hbm.at[:, lo:hi], sems.at[8 + i])
        c.start()
        done.append(c)
    kept.wait()
    for c in done:
        c.wait()


SPECS = {
    "v": pl.BlockSpec(memory_space=pltpu.VMEM),
    "s": pl.BlockSpec(memory_space=pltpu.SMEM),
    "a": pl.BlockSpec(memory_space=pl.ANY),
}


def call(kernel, ins, outs, spec, scratch, args, limit, copies=0, flops=int(1e9), alias={}):
    shapes = [jax.ShapeDtypeStruct(o, jnp.int32 if c == "s" else F32) for o, c in zip(outs, spec)]
    moved = sum(a.size * a.dtype.itemsize for a in args) + sum(4 * int(np.prod(o)) for o in outs)
    scratch = [x if not isinstance(x, tuple) else pltpu.VMEM(x, F32) for x in scratch]
    return pl.pallas_call(
        kernel,
        out_shape=shapes if len(outs) > 1 else shapes[0],
        in_specs=[SPECS[c] for c in ins],
        out_specs=[SPECS[c] for c in spec] if len(outs) > 1 else SPECS[spec],
        scratch_shapes=scratch + ([pltpu.SemaphoreType.DMA((copies,))] if copies else []),
        input_output_aliases=alias,
        compiler_params=pltpu.CompilerParams(vmem_limit_bytes=limit << 20),
        cost_estimate=pl.CostEstimate(flops=flops, bytes_accessed=moved, transcendentals=0),
        name=kernel.__name__.removesuffix("_kernel"),
    )(*args)


def shifted(block, distance):
    devices = range(lax.axis_size("sfc"))
    return lax.ppermute(block, "sfc", [(i, i + distance) for i in devices if i + distance in devices])


def exchange(block):
    return lax.all_to_all(block, "node", 0, 0, tiled=True)


def gathered(note, packed, first, second):
    me = lax.axis_index("node")
    parents = note[:, 6]
    parent = parents[me]
    ring = [(i, (i + 1) % PIECES) for i in range(PIECES)]
    size = 6 * FACE

    def faces_step(i, held):
        faces, ghost = held
        owner = (me - i) % PIECES
        mine = lax.dynamic_slice(faces, (parent % 8 * size, 0), (size, 128))
        ghost = jnp.where(parent // 8 == owner, mine, ghost)
        return lax.ppermute(faces, "node", ring), ghost

    _, ghost = lax.fori_loop(0, PIECES, faces_step, (packed[: 8 * size], jnp.zeros((size, 128), F32)))

    def flux_step(i, held):
        flux, rows = held
        box = (me - i) % PIECES
        at = (parents[box] % 8 * size, 0)
        added = lax.dynamic_slice(rows, at, (size, 128)) + flux
        return lax.ppermute(flux, "node", ring), jnp.where(parents[box] // 8 == me, lax.dynamic_update_slice(rows, added, at), rows)

    flux = first.reshape(size, 128) - second.reshape(size, 128) * ghost
    _, rows = lax.fori_loop(0, PIECES, flux_step, (flux, jnp.zeros((8 * size, 128), F32)))
    return ghost.reshape(6, FACE, 128), rows


def local(fine_state, conduct, spec_rate, reaction, coarse_state, ghost_source, parent_box):
    pick = jnp.asarray(pick_fine(), BF16)
    mean = jnp.asarray(average(), BF16)
    box = (1, S, B, AREA)
    fine, weighted = call(
        pack_fine_kernel,
        "aaaaa",
        [(PIECES, FINE, 128), (12 * SLOTS, 512)],
        "aa",
        [
            pltpu.SMEM((1, 6), jnp.int32), pltpu.SMEM((1,), jnp.int32), box, (1, B, AREA),
            pltpu.VMEM((AREA, 128), BF16), (PIECES, FINE, 128), (12 * SLOTS, 512), (SLOTS * 32, 128), (2, SLOTS, AREA),
        ],
        (ghost_source, parent_box, fine_state, conduct, pick),
        58,
        17,
    )
    own = exchange(fine)
    packed, first, second = call(
        pack_coarse_kernel,
        "aaaaaaa",
        [(48 * FACE + PIECES * MEANS, 128), (6, FACE, 128), (6, FACE, 128)],
        "aaa",
        [
            pltpu.SMEM((S,), F32), pltpu.SMEM((1, 6), jnp.int32), box, (12 * SLOTS, 512),
            pltpu.VMEM((AREA, 256), BF16), pltpu.VMEM((256, 256), BF16), pltpu.VMEM((512, 128), BF16),
            (2, S * 32, 128), (4 * SLOTS, AREA), (48 * FACE + PIECES * MEANS, 128), (6, FACE, 128), (6, FACE, 128),
        ],
        (spec_rate, ghost_source, coarse_state, weighted, jnp.asarray(pick_coarse(), BF16), jnp.asarray(split_octants(), BF16), mean),
        58,
        13,
    )
    note = own[:, 11, :8].astype(jnp.int32)
    coarse, listed = call(
        choose_kernel,
        "sv",
        [(PIECES, LIST + MEANS, 128), (CAP + 1,)],
        "as",
        [(PIECES, LIST + MEANS, 128), pltpu.SMEM((1,), jnp.int32)],
        (note, packed),
        24,
        1,
    )
    before, after = shifted(own, 1), shifted(own, -1)
    grouped = exchange(coarse)
    chosen, plan = call(
        relay_kernel,
        "sssvvvv",
        [(PIECES, FINE + LIST, 128), (1 + CAP + 6,)],
        "as",
        [
            (PIECES, FINE + LIST, 128), (3 * 96, ROWS, 128), (PIECES * CAP, PART, 128), (PIECES * CAP + 1, PART, 128),
            pltpu.SMEM((PIECES,), jnp.int32),
        ],
        (note, listed, spec_rate, before, own, after, grouped),
        24,
        2,
    )
    mine = exchange(chosen)
    inner = call(inner_kernel, "svvva", [(1, S + 1, B, AREA)], "v", [(7, B, AREA)], (spec_rate, fine_state, conduct, reaction, chosen), 24)
    ghost, rows = lax.cond(
        plan[0] > 0,
        gathered,
        lambda note, packed, first, second: (first, packed[: 48 * FACE]),
        note, packed, first, second,
    )
    tendency, register = call(
        outer_kernel,
        "ssvvaa",
        [box, (1, S, 48, 256)],
        "aa",
        [
            box, (1, S, 48, 256),
            (6, FACE, 128), (12 * SLOTS, 128), (12 * SLOTS, 512), (2, SLOTS, AREA), (SLOTS * 32, 128), (49 * FACE, 128), (CAP, FACE, 128),
        ],
        (spec_rate, plan, mine, inner, ghost, rows),
        28,
        14,
    )
    return tendency, register.transpose(0, 2, 1, 3)


def solution(mesh):
    box = P(("sfc", "node"))
    return jax.shard_map(
        local,
        mesh=mesh,
        in_specs=(box, box, P(), P(), box, box, box),
        out_specs=(box, box),
        check_vma=False,
    )
```
